128 devices in a mesh: lat: 16 (over z, x), lon: 8 (over y, core).
Axes of the slice: x: 4, y: 4, z: 4, core: 2. Of those that a mesh axis runs over, the one named last changes fastest.
Arguments:
- field: bfloat16 [69, 512, 4096], P(None, 'lat', 'lon'), may hold values from -6 to 6
- stem_weight: bfloat16 [1104, 512], replicated, may hold values from -0.1875 to 0.1875
- stem_bias: float32 [512], replicated, may hold values from -3 to 3
- token_gain: float32 [512], replicated, may hold values from 0.1 to 1.9
- kv_weight: bfloat16 [512, 1024], replicated, may hold values from -0.25 to 0.25
- latents: float32 [512, 512], replicated, may hold values from -6 to 6
- latent_gain: float32 [512], replicated, may hold values from 0.1 to 1.9
- query_weight: bfloat16 [512, 512], replicated, may hold values from -0.25 to 0.25
- head_gain: float32 [8], replicated, may hold values from 2 to 40
- out_weight: bfloat16 [512, 512], replicated, may hold values from -0.25 to 0.25
- out_gain: float32 [512], replicated, may hold values from 0.1 to 1.9
Outputs:
- tokens: bfloat16 [256, 2048, 512], P('lat', 'lon')
- latent_out: float32 [512, 512], replicated
The draws below stay inside these ranges and needn't reach their ends.
All inputs are finite; a program needn't handle non-finite values.
Results may differ from the reference program's by a relative error of at most 0.015.
The reference program's roundings to bfloat16 on the way count: a program that leaves them out, or rounds other values in their place, can miss the bound.
Values may be sent and summed in bfloat16 or wider, within the bound.
A program may use at most 512 MiB of HBM per device.

```python
import jax
import jax.numpy as jnp
from jax import lax

CHAN = 69
D = 512
HEADS = 8
HD = 64
LAT = 512
TH = 16
NLAT = 512
NLON = 4096
NTW = 2048
N_LAT = 16


def draw_head_gain(key, part):
    return jnp.exp(jax.random.uniform(key, (HEADS,), jnp.float32, jnp.log(2.0), jnp.log(24.0)))


def steps_of(rng, extent, cuts, smallest, high):
    def one(dim, blocks):
        draws = jax.random.uniform(jax.random.fold_in(jax.random.fold_in(rng, 6), dim), (blocks,), jnp.float32, smallest / len(cuts), high / len(cuts))
        return jnp.repeat(jnp.exp(draws), extent[dim] // blocks).reshape((-1,) + (1,) * (len(extent) - dim - 1))

    level = one(*cuts[0])
    for cut in cuts[1:]:
        level = level * one(*cut)
    return level


def scatter_about(own_key, extent, scale, most, cuts=(), dtype=jnp.bfloat16):
    level = steps_of(own_key, extent, cuts, -0.22, 0.18) if cuts else 1.0
    array = jax.random.normal(own_key, extent, jnp.float32) * scale * level
    return jnp.minimum(jnp.maximum(array, -most), most).astype(dtype)


def setup_inputs(seed: int = 0) -> dict:
    key_of = jax.random.split(jax.random.key(seed), 12)
    field = scatter_about(key_of[0], (CHAN, NLAT, NLON), 1.0, 6.0, ((1, 16), (2, 8)))
    stem_weight = scatter_about(key_of[1], (16 * CHAN, D), (16 * CHAN) ** -0.5, 0.1875)
    stem_bias = scatter_about(key_of[2], (D,), 0.5, 3.0, (), jnp.float32)
    token_gain = jnp.clip(1.0 + 0.18 * jax.random.normal(key_of[3], (D,), jnp.float32), 0.1, 1.9)
    kv_weight = scatter_about(key_of[4], (D, 2 * D), D ** -0.5, 0.25)
    latents = scatter_about(key_of[5], (LAT, D), 1.0, 6.0, (), jnp.float32)
    latent_gain = jnp.clip(1.0 + 0.18 * jax.random.normal(key_of[6], (D,), jnp.float32), 0.1, 1.9)
    query_weight = scatter_about(key_of[7], (D, D), D ** -0.5, 0.25)
    head_gain = draw_head_gain(jax.random.fold_in(key_of[11], 71), 0)
    out_weight = scatter_about(key_of[9], (D, D), D ** -0.5, 0.25)
    out_gain = jnp.clip(1.0 + 0.18 * jax.random.normal(key_of[10], (D,), jnp.float32), 0.1, 1.9)
    return {"field": field, "stem_weight": stem_weight, "stem_bias": stem_bias, "token_gain": token_gain, "kv_weight": kv_weight, "latents": latents, "latent_gain": latent_gain, "query_weight": query_weight, "head_gain": head_gain, "out_weight": out_weight, "out_gain": out_gain}


def normalize(values):
    mean = lax.optimization_barrier(jnp.mean(values, axis=-1, keepdims=True))
    centred = values - mean
    spread = lax.optimization_barrier(jnp.mean(centred * centred, axis=-1, keepdims=True))
    return centred / jnp.sqrt(spread + 1e-05)

def reference(field, stem_weight, stem_bias, token_gain, kv_weight, latents, latent_gain, query_weight, head_gain, out_weight, out_gain):
    widened = jnp.concatenate([field[:, :, -1:], field, field[:, :, :1]], axis=2)
    widened = jnp.pad(widened, ((0, 0), (1, 1), (0, 0)))
    kernel = stem_weight.reshape(4, 4, CHAN, D)
    stem = lax.conv_general_dilated(widened[None], kernel, (2, 2), 'VALID', dimension_numbers=('NCHW', 'HWIO', 'NHWC'), preferred_element_type=jnp.float32)[0]
    tokens = (normalize(stem + stem_bias) * token_gain).astype(jnp.bfloat16)
    normed = (normalize(latents) * latent_gain).astype(jnp.bfloat16)
    query = jnp.dot(normed, query_weight, preferred_element_type=jnp.float32).astype(jnp.bfloat16)
    query_heads = query.reshape(LAT, HEADS, HD).astype(jnp.float32)
    factor = head_gain / jnp.sqrt(jnp.float32(HD))
    bands = tokens.reshape(N_LAT, TH * NTW, D)

    def attend(carry, band):
        peak, total, accum = carry
        kv = jnp.dot(band, kv_weight, preferred_element_type=jnp.float32).astype(jnp.bfloat16)
        keys = kv[:, :D].reshape(-1, HEADS, HD).astype(jnp.float32)
        values = kv[:, D:].reshape(-1, HEADS, HD).astype(jnp.float32)
        scores = jnp.einsum('ihd,thd->hit', query_heads, keys, precision=lax.Precision.HIGHEST) * factor[:, None, None]
        newpeak = jnp.maximum(peak, lax.optimization_barrier(jnp.max(scores, axis=-1)))
        fold = jnp.exp(peak - newpeak)
        expo = jnp.exp(scores - newpeak[:, :, None])
        total = total * fold + lax.optimization_barrier(jnp.sum(expo, axis=-1))
        rounded = expo.astype(jnp.bfloat16).astype(jnp.float32)
        part = jnp.einsum('hit,thd->ihd', rounded, values, precision=lax.Precision.HIGHEST)
        accum = accum * jnp.transpose(fold)[:, :, None] + part
        return ((newpeak, total, accum), None)
    start = (jnp.full((HEADS, LAT), -1e+30, jnp.float32), jnp.zeros((HEADS, LAT), jnp.float32), jnp.zeros((LAT, HEADS, HD), jnp.float32))
    (peak, total, accum), unused = lax.scan(attend, start, bands)
    attended = (accum / jnp.transpose(total)[:, :, None]).reshape(LAT, D).astype(jnp.bfloat16)
    mixed = jnp.dot(attended, out_weight, preferred_element_type=jnp.float32)
    latent_out = normalize(mixed) * out_gain
    return (tokens, latent_out)
```

```python
import functools

import jax
import jax.numpy as jnp
from jax import lax
from jax.experimental import pallas as pl
from jax.experimental.pallas import tpu as pltpu
from jax.sharding import PartitionSpec as P

HEADS = 8
HD = 64
LAT = 512
D = 512
CHAN = 69
CPAD = 80
ROWS = 32
COLS = 512
TH = 16
TW = 256
TOK = TH * TW
SLAB = 4 * CPAD
NLATD = 16
NLOND = 8
EXT = 80
CH = 1024
MESH = pl.DeviceIdType.MESH
F32 = jnp.float32
BF = jnp.bfloat16
VM = pl.BlockSpec(memory_space=pltpu.VMEM)
SM = pl.BlockSpec(memory_space=pltpu.SMEM)
ANY = pl.BlockSpec(memory_space=pl.ANY)


def remote(src, dst, send, recv, target):
    return pltpu.make_async_remote_copy(
        src_ref=src, dst_ref=dst, send_sem=send, recv_sem=recv, device_id=target, device_id_type=MESH
    )


def prep_kernel(
    field_ref, sw_ref, kvw_ref, latents_ref, lgain_ref, qw_ref,
    sl_ref, wt_ref, wvt_ref, qt_ref,
    g_ref, wf_ref, wp_ref, cols_ref, colr_ref, rowr_ref, send_sem, recv_sem,
):
    lat = lax.axis_index("lat")
    lon = lax.axis_index("lon")
    up, down = lax.rem(lat + NLATD - 1, NLATD), lax.rem(lat + 1, NLATD)
    left, right = lax.rem(lon + NLOND - 1, NLOND), lax.rem(lon + 1, NLOND)
    barrier = pltpu.get_barrier_semaphore()
    around = [(lat, left), (lat, right), (up, lon), (down, lon), (up, left), (up, right), (down, left), (down, right)]
    for target in around:
        pl.semaphore_signal(barrier, inc=1, device_id=target, device_id_type=MESH)

    source = lax.broadcasted_iota(jnp.int32, (256, 256), 0)
    place = lax.broadcasted_iota(jnp.int32, (256, 256), 1)
    wanted = jnp.where(place < 128, 2 * place, 2 * (place - 128) + 1)
    select = (source == wanted).astype(F32).astype(BF)
    for half in range(2):
        block = field_ref[:, :, half * 256:(half + 1) * 256].reshape(CHAN * ROWS, 256)
        both = jnp.dot(block, select, preferred_element_type=F32)
        g_ref[half, 0:CHAN * ROWS, :] = both[:, :128]
        g_ref[2 + half, 0:CHAN * ROWS, :] = both[:, 128:]
    g_ref[:, CHAN * ROWS:CPAD * ROWS, :] = jnp.zeros((4, (CPAD - CHAN) * ROWS, 128), F32)

    lane = lax.broadcasted_iota(jnp.int32, (CPAD, 128), 1)

    def spread(y, carry):
        first, last = carry
        quarter = [g_ref[n, pl.ds(y, CPAD, stride=ROWS), :] for n in range(4)]
        even = jnp.concatenate(quarter[:2], axis=1)
        odd = jnp.concatenate(quarter[2:], axis=1)
        base = pl.multiple_of((y + 1) * SLAB, SLAB)
        sl_ref[pl.ds(base, CPAD), :] = pltpu.roll(odd, 1, 1).astype(BF)
        sl_ref[pl.ds(base + CPAD, CPAD), :] = even.astype(BF)
        sl_ref[pl.ds(base + 2 * CPAD, CPAD), :] = odd.astype(BF)
        sl_ref[pl.ds(base + 3 * CPAD, CPAD), :] = pltpu.roll(even, 255, 1).astype(BF)
        first = jnp.where(lane == y, pltpu.roll(even[:, :128], y, 1), first)
        last = jnp.where(lane == y, pltpu.roll(odd[:, 128:], y + 1, 1), last)
        return first, last

    empty = jnp.zeros((CPAD, 128), F32)
    first, last = lax.fori_loop(0, ROWS, spread, (empty, empty))
    cols_ref[0] = first.astype(BF)
    cols_ref[1] = last.astype(BF)
    pl.semaphore_wait(barrier, 8)
    routes = [
        (cols_ref.at[1], colr_ref.at[0], (lat, right)),
        (cols_ref.at[0], colr_ref.at[1], (lat, left)),
        (cols_ref.at[1], colr_ref.at[2], (down, right)),
        (cols_ref.at[0], colr_ref.at[3], (down, left)),
        (cols_ref.at[1], colr_ref.at[4], (up, right)),
        (cols_ref.at[0], colr_ref.at[5], (up, left)),
        (sl_ref.at[pl.ds(ROWS * SLAB + CPAD, 2 * CPAD)], rowr_ref.at[0], (down, lon)),
        (sl_ref.at[pl.ds(SLAB + CPAD, 2 * CPAD)], rowr_ref.at[1], (up, lon)),
    ]
    copies = [
        remote(src, dst, send_sem.at[i], recv_sem.at[i], target)
        for i, (src, dst, target) in enumerate(routes)
    ]
    for i in (6, 7, 0, 1, 2, 3, 4, 5):
        copies[i].start()

    wf_ref[...] = sw_ref[...].astype(F32)
    for q in range(16):
        part = wf_ref[pl.ds(q * CHAN, CHAN), :]
        part = jnp.concatenate([part, jnp.zeros((CPAD - CHAN, D), F32)], axis=0)
        wp_ref[pl.ds(q * CPAD, CPAD), :] = part.astype(BF)
    for q in range(5):
        wt_ref[:, pl.ds(q * 256, 256)] = wp_ref[pl.ds(q * 256, 256), :].T
    wvt_ref[...] = kvw_ref[:, D:].T
    latents = latents_ref[...]
    centred = latents - jnp.mean(latents, axis=-1, keepdims=True)
    variance = jnp.mean(centred * centred, axis=-1, keepdims=True)
    normed = (centred / jnp.sqrt(variance + 1e-05) * lgain_ref[...]).astype(BF)
    query = jnp.dot(normed, qw_ref[...], preferred_element_type=F32).astype(BF)
    turned = query.T
    for h in range(HEADS):
        mine = (h % 2) * HD
        qt_ref[h, mine:mine + HD, :] = turned[h * HD:(h + 1) * HD, :]
        qt_ref[h, HD - mine:2 * HD - mine, :] = jnp.zeros((HD, LAT), BF)

    for copy in copies:
        copy.wait()

    def patch(y, left_column, right_column, left_roll, right_roll, base):
        a = sl_ref[pl.ds(base, CPAD), 0:128].astype(F32)
        b = sl_ref[pl.ds(base + 3 * CPAD, CPAD), 128:256].astype(F32)
        low = pltpu.roll(left_column.astype(F32), left_roll, 1)
        high = pltpu.roll(right_column.astype(F32), right_roll, 1)
        sl_ref[pl.ds(base, CPAD), 0:128] = jnp.where(lane == 0, low, a).astype(BF)
        sl_ref[pl.ds(base + 3 * CPAD, CPAD), 128:256] = jnp.where(lane == 127, high, b).astype(BF)

    def mend(y, carry):
        base = pl.multiple_of((y + 1) * SLAB, SLAB)
        patch(y, colr_ref[0], colr_ref[1], lax.rem(128 - y, 128), 127 - y, base)
        return carry

    lax.fori_loop(0, ROWS, mend, 0)
    for index, (slab, y, inside) in enumerate([(0, ROWS - 1, lat > 0), (ROWS + 1, 0, lat < NLATD - 1)]):
        base = slab * SLAB
        keep = jnp.where(inside, 1.0, 0.0).astype(F32)
        even = rowr_ref[index, 0:CPAD, :].astype(F32) * keep
        odd = rowr_ref[index, CPAD:2 * CPAD, :].astype(F32) * keep
        sl_ref[pl.ds(base, CPAD), :] = pltpu.roll(odd, 1, 1).astype(BF)
        sl_ref[pl.ds(base + CPAD, CPAD), :] = even.astype(BF)
        sl_ref[pl.ds(base + 2 * CPAD, CPAD), :] = odd.astype(BF)
        sl_ref[pl.ds(base + 3 * CPAD, CPAD), :] = pltpu.roll(even, 255, 1).astype(BF)
        patch(
            y, colr_ref[2 + 2 * index].astype(F32) * keep, colr_ref[3 + 2 * index].astype(F32) * keep,
            (128 - y) % 128, 127 - y, base,
        )


def prep(field, sw, kvw, latents, lgain, qw):
    return pl.pallas_call(
        prep_kernel,
        out_shape=(
            jax.ShapeDtypeStruct(((ROWS + 2) * SLAB, TW), BF),
            jax.ShapeDtypeStruct((D, 16 * CPAD), BF),
            jax.ShapeDtypeStruct((D, D), BF),
            jax.ShapeDtypeStruct((HEADS, 2 * HD, LAT), BF),
        ),
        in_specs=[VM] * 6,
        out_specs=(VM,) * 4,
        scratch_shapes=[
            pltpu.VMEM((4, CPAD * ROWS, 128), F32),
            pltpu.VMEM((16 * CHAN, D), F32),
            pltpu.VMEM((16 * CPAD, D), BF),
            pltpu.VMEM((2, CPAD, 128), BF),
            pltpu.VMEM((6, CPAD, 128), BF),
            pltpu.VMEM((2, 2 * CPAD, TW), BF),
            pltpu.SemaphoreType.DMA((8,)),
            pltpu.SemaphoreType.DMA((8,)),
        ],
        compiler_params=pltpu.CompilerParams(
            collective_id=0, has_side_effects=True, vmem_limit_bytes=56 * 2**20
        ),
        name="prep",
    )(field, sw, kvw, latents, lgain, qw)


def token_kernel(low_ref, high_ref, wt_ref, bias_ref, gain_ref, kvw_ref, wvt_ref, tok_ref, k_ref, vt_ref):
    window = jnp.concatenate([low_ref[...], high_ref[...]], axis=0)
    stem = jnp.dot(wt_ref[...], window, preferred_element_type=F32) + bias_ref[...]
    centred = stem - jnp.mean(stem, axis=0, keepdims=True)
    variance = jnp.mean(centred * centred, axis=0, keepdims=True)
    turned = (centred / jnp.sqrt(variance + 1e-05) * gain_ref[...]).astype(BF)
    tokens = turned.T
    tok_ref[0] = tokens
    keys = jnp.dot(tokens, kvw_ref[...], preferred_element_type=F32).astype(BF)
    for pair in range(HEADS // 2):
        k_ref[pair] = keys[:, pair * 128:(pair + 1) * 128]
    values = jnp.dot(wvt_ref[...], turned, preferred_element_type=F32).astype(BF)
    for h in range(HEADS):
        vt_ref[h, 0:HD, :] = values[h * HD:(h + 1) * HD, :]
        vt_ref[h, HD:EXT, :] = jnp.ones((EXT - HD, TW), BF)


def tokenise(slabs, wt, bias, gain, kvw, wvt):
    fixed = lambda shape: pl.BlockSpec(shape, lambda r: (0,) * len(shape))
    return pl.pallas_call(
        token_kernel,
        grid=(TH,),
        out_shape=(
            jax.ShapeDtypeStruct((TH, TW, D), BF),
            jax.ShapeDtypeStruct((HEADS // 2, TOK, 128), BF),
            jax.ShapeDtypeStruct((HEADS, EXT, TOK), BF),
        ),
        in_specs=[
            pl.BlockSpec((2 * SLAB, TW), lambda r: (r, 0)),
            pl.BlockSpec((2 * SLAB, TW), lambda r: (r + 1, 0)),
            fixed((D, 16 * CPAD)),
            fixed((D, 1)),
            fixed((D, 1)),
            fixed((D, D)),
            fixed((D, D)),
        ],
        out_specs=(
            pl.BlockSpec((1, TW, D), lambda r: (r, 0, 0)),
            pl.BlockSpec((HEADS // 2, TW, 128), lambda r: (0, r, 0)),
            pl.BlockSpec((HEADS, EXT, TW), lambda r: (0, 0, r)),
        ),
        compiler_params=pltpu.CompilerParams(vmem_limit_bytes=56 * 2**20),
        name="tokenise",
    )(slabs, slabs, wt, bias, gain, kvw, wvt)


def attend_kernel(
    k_hbm, vt_hbm, qt_hbm, hg_ref, out_ref,
    k_ref, vt_ref, qt_ref, s_ref, mx_ref, acc_ref, src1, dst1, src2, dst2, att,
    in_sem, send1, recv1, send2, recv2, send3, recv3,
):
    lat = lax.axis_index("lat")
    lon = lax.axis_index("lon")
    barrier = pltpu.get_barrier_semaphore()
    lon_peer = lambda s: (lat, lax.rem(lon + s, NLOND))
    lat_peer = lambda s: (lax.rem(lat + s, NLATD), lon)
    for s in range(1, NLOND):
        pl.semaphore_signal(barrier, inc=1, device_id=lon_peer(s), device_id_type=MESH)
    for s in range(1, NLATD):
        pl.semaphore_signal(barrier, inc=1, device_id=lat_peer(s), device_id_type=MESH)

    qt_copy = pltpu.make_async_copy(qt_hbm, qt_ref, in_sem.at[12])
    k_copies = [pltpu.make_async_copy(k_hbm.at[p], k_ref.at[p], in_sem.at[p]) for p in range(HEADS // 2)]
    v_copies = [pltpu.make_async_copy(vt_hbm.at[h], vt_ref.at[h], in_sem.at[4 + h]) for h in range(HEADS)]
    qt_copy.start()
    k_copies[0].start()
    v_copies[0].start()
    v_copies[1].start()
    for p in range(1, HEADS // 2):
        k_copies[p].start()
        v_copies[2 * p].start()
        v_copies[2 * p + 1].start()

    log2e = 1.4426950408889634
    scale = lambda h: hg_ref[h] * (log2e / 8.0)

    def score(h, j):
        at = pl.ds(pl.multiple_of(j * CH, CH), CH)
        s = jnp.dot(k_ref[h // 2, at, :], qt_ref[h], preferred_element_type=F32)
        s_ref[h % 2, at, :] = s
        mx_ref[h % 2] = jnp.maximum(mx_ref[h % 2], jnp.max(s.reshape(CH // 8, 8, LAT), axis=0))

    def weigh(h, j, top):
        at = pl.ds(pl.multiple_of(j * CH, CH), CH)
        p = jnp.exp2(s_ref[h % 2, at, :] * scale(h) - top).astype(BF)
        acc_ref[...] += jnp.dot(vt_ref[h, :, at], p, preferred_element_type=F32)

    def stat_rows(top, total):
        row = lax.broadcasted_iota(jnp.int32, (16, 128), 0)
        high = total.astype(BF).astype(F32)
        out = jnp.zeros((16, 128), F32)
        for n, value in enumerate((top, high, total - high)):
            out = jnp.where(row == 2 * n, value[:, :128], out)
            out = jnp.where(row == 2 * n + 1, value[:, 128:], out)
        return out.astype(BF)

    def merge(buffer, h, count):
        stats = [buffer[h, s, :, 256:384].astype(F32) for s in range(count)]
        tops = [jnp.concatenate([x[0:1], x[1:2]], axis=1) for x in stats]
        totals = [jnp.concatenate([x[2:3] + x[4:5], x[3:4] + x[5:6]], axis=1) for x in stats]
        top = functools.reduce(jnp.maximum, tops)
        total = jnp.zeros((1, 256), F32)
        acc = jnp.zeros((16, 256), F32)
        for s in range(count):
            fold = jnp.exp2(tops[s] - top)
            total = total + totals[s] * fold
            acc = acc + buffer[h, s, :, 0:256].astype(F32) * fold
        return top, total, acc

    def stage1(h, top):
        acc = acc_ref[...]
        total = acc[HD:HD + 1, :]
        stats = [stat_rows(top[:, g * 256:(g + 1) * 256], total[:, g * 256:(g + 1) * 256]) for g in range(2)]
        for p in range(NLOND):
            e, g = p % 4, p // 4
            src1[h, p, :, 0:256] = acc[16 * e:16 * e + 16, g * 256:(g + 1) * 256].astype(BF)
            src1[h, p, :, 256:384] = stats[g]
        dst1[h, 0] = src1[h, lon]
        for s in range(1, NLOND):
            remote(src1.at[h, lax.rem(lon + s, NLOND)], dst1.at[h, s], send1.at[h], recv1.at[h], lon_peer(s)).start()

    def wait(ref, sem):
        pltpu.make_async_copy(ref, ref, sem).wait()

    def stage2(h):
        wait(dst1.at[h, pl.ds(1, NLOND - 1)], recv1.at[h])
        top, total, acc = merge(dst1, h, NLOND)
        stats = stat_rows(top, total)
        src2[h, :, 0:256] = acc.astype(BF)
        src2[h, :, 256:384] = stats
        dst2[h, 0, :, 0:256] = acc.astype(BF)
        dst2[h, 0, :, 256:384] = stats
        for s in range(1, NLATD):
            remote(src2.at[h], dst2.at[h, s], send2.at[h], recv2.at[h], lat_peer(s)).start()

    e_at = lax.rem(lon, 4) * 16
    g_at = pl.multiple_of(lon // 4 * 256, 256)

    def stage3(h):
        wait(dst2.at[h, pl.ds(1, NLATD - 1)], recv2.at[h])
        top, total, acc = merge(dst2, h, NLATD)
        here = att.at[pl.ds(pl.multiple_of(h * HD + e_at, 16), 16), pl.ds(g_at, 256)]
        here[...] = (acc / total).astype(BF)
        for s in range(1, NLOND):
            remote(here, here, send3.at[h], recv3.at[h], lon_peer(s)).start()

    for h in range(HEADS + 1):
        slot = h % 2
        if h < HEADS:
            if h == 0:
                qt_copy.wait()
            if h % 2 == 0:
                k_copies[h // 2].wait()
            mx_ref[slot] = jnp.full((8, LAT), -jnp.inf, F32)
        if h > 0:
            v_copies[h - 1].wait()
            peak = jnp.max(mx_ref[1 - slot], axis=0, keepdims=True) * scale(h - 1)
            top = (peak + jnp.abs(peak) * 2.0**-7).astype(BF).astype(F32)
            acc_ref[...] = jnp.zeros_like(acc_ref)

        def both(j, carry):
            if h < HEADS:
                score(h, j)
            if h > 0:
                weigh(h - 1, j, top)
            return carry

        lax.fori_loop(0, TOK // CH, both, 0)
        if h == 1:
            pl.semaphore_wait(barrier, NLOND + NLATD - 2)
        if h > 0:
            stage1(h - 1, top)
        if h > 1:
            stage2(h - 2)
        if h > 2:
            stage3(h - 3)
    stage2(HEADS - 1)
    stage3(HEADS - 2)
    stage3(HEADS - 1)
    for h in range(HEADS):
        wait(att.at[pl.ds(0, 112), pl.ds(0, 256)], recv3.at[h])
        wait(dst1.at[h, pl.ds(1, NLOND - 1)], send1.at[h])
        wait(dst2.at[h, pl.ds(1, NLATD - 1)], send2.at[h])
        wait(att.at[pl.ds(0, 112), pl.ds(0, 256)], send3.at[h])
    out_ref[...] = att[...]


def attend(k, vt, qt, hg):
    return pl.pallas_call(
        attend_kernel,
        out_shape=jax.ShapeDtypeStruct((D, LAT), BF),
        in_specs=[ANY, ANY, ANY, SM],
        out_specs=VM,
        scratch_shapes=[
            pltpu.VMEM((HEADS // 2, TOK, 128), BF),
            pltpu.VMEM((HEADS, EXT, TOK), BF),
            pltpu.VMEM((HEADS, 2 * HD, LAT), BF),
            pltpu.VMEM((2, TOK, LAT), F32),
            pltpu.VMEM((2, 8, LAT), F32),
            pltpu.VMEM((EXT, LAT), F32),
            pltpu.VMEM((HEADS, NLOND, 16, 384), BF),
            pltpu.VMEM((HEADS, NLOND, 16, 384), BF),
            pltpu.VMEM((HEADS, 16, 384), BF),
            pltpu.VMEM((HEADS, NLATD, 16, 384), BF),
            pltpu.VMEM((D, LAT), BF),
            pltpu.SemaphoreType.DMA((13,)),
        ] + [pltpu.SemaphoreType.DMA((HEADS,))] * 6,
        compiler_params=pltpu.CompilerParams(
            collective_id=1, has_side_effects=True, vmem_limit_bytes=56 * 2**20
        ),
        name="attend",
    )(k, vt, qt, hg)


def mix_kernel(att_ref, ow_ref, gain_ref, out_ref):
    mixed = lax.dot_general(
        att_ref[...], ow_ref[...], (((0,), (0,)), ((), ())), preferred_element_type=F32
    )
    centred = mixed - jnp.mean(mixed, axis=-1, keepdims=True)
    variance = jnp.mean(centred * centred, axis=-1, keepdims=True)
    out_ref[...] = centred / jnp.sqrt(variance + 1e-05) * gain_ref[...]


def mix(att, ow, gain):
    return pl.pallas_call(
        mix_kernel,
        out_shape=jax.ShapeDtypeStruct((LAT, D), F32),
        in_specs=[VM] * 3,
        out_specs=VM,
        name="mix",
    )(att, ow, gain)


def shards(
    field, stem_weight, stem_bias, token_gain, kv_weight, latents, latent_gain,
    query_weight, head_gain, out_weight, out_gain,
):
    slabs, wt, wvt, qt = prep(field, stem_weight, kv_weight, latents, latent_gain.reshape(1, D), query_weight)
    tokens, k, vt = tokenise(
        slabs, wt, stem_bias.reshape(D, 1), token_gain.reshape(D, 1), kv_weight, wvt
    )
    att = attend(k, vt, qt, head_gain)
    return tokens, mix(att, out_weight, out_gain.reshape(1, D))


def solution(mesh):
    return jax.shard_map(
        shards,
        mesh=mesh,
        in_specs=(P(None, "lat", "lon"), P(), P(), P(), P(), P(), P(), P(), P(), P(), P()),
        out_specs=(P("lat", "lon", None), P()),
        check_vma=False,
    )
```

```python
import functools

import jax
import jax.numpy as jnp
from jax import lax
from jax.experimental import pallas as pl
from jax.experimental.pallas import tpu as pltpu
from jax.sharding import PartitionSpec as P

HEADS = 8
HD = 64
LAT = 512
D = 512
CHAN = 69
CPAD = 80
ROWS = 32
COLS = 512
TH = 16
TW = 256
TOK = TH * TW
SLAB = 4 * CPAD
NLATD = 16
NLOND = 8
EXT = 80
CH = 2048
PITCH = 40
MESH = pl.DeviceIdType.MESH
F32 = jnp.float32
BF = jnp.bfloat16
VM = pl.BlockSpec(memory_space=pltpu.VMEM)
SM = pl.BlockSpec(memory_space=pltpu.SMEM)
ANY = pl.BlockSpec(memory_space=pl.ANY)


def remote(src, dst, send, recv, target):
    return pltpu.make_async_remote_copy(
        src_ref=src, dst_ref=dst, send_sem=send, recv_sem=recv, device_id=target, device_id_type=MESH
    )


def encode_kernel(
    field_hbm, sw_hbm, kvw_hbm, latents_hbm, qw_hbm, bias_ref, gain_ref, lgain_ref, hg_ref,
    tok_hbm, out_ref,
    field_ref, sw_ref, kvw_ref, latents_ref, qw_ref,
    sl_ref, wt_ref, wvt_ref, qt_ref, g_ref, wp_ref, cols_ref, colr_ref, rowr_ref,
    affine_ref, stem_ref, tok_ref,
    k_ref, vt_ref, s_ref, mx_ref, acc_ref, src1, dst1, src2, dst2, att,
    in_sem, tok_sem, edge_send, edge_recv, send1, recv1, send2, recv2, send3, recv3,
):
    lat = lax.axis_index("lat")
    lon = lax.axis_index("lon")
    up, down = lax.rem(lat + NLATD - 1, NLATD), lax.rem(lat + 1, NLATD)
    left, right = lax.rem(lon + NLOND - 1, NLOND), lax.rem(lon + 1, NLOND)
    loads = [
        pltpu.make_async_copy(src, dst, in_sem.at[i])
        for i, (src, dst) in enumerate([
            (field_hbm, field_ref), (sw_hbm, sw_ref), (kvw_hbm, kvw_ref), (latents_hbm, latents_ref), (qw_hbm, qw_ref),
        ])
    ]
    for load in loads:
        load.start()
    lon_peer = lambda s: (lat, lax.rem(lon + s, NLOND))
    lat_peer = lambda s: (lax.rem(lat + s, NLATD), lon)
    barrier = pltpu.get_barrier_semaphore()
    around = [(up, left), (up, right), (down, left), (down, right)]
    around += [lon_peer(s) for s in range(1, NLOND)] + [lat_peer(s) for s in range(1, NLATD)]
    for target in around:
        pl.semaphore_signal(barrier, inc=1, device_id=target, device_id_type=MESH)

    source = lax.broadcasted_iota(jnp.int32, (256, 256), 0)
    place = lax.broadcasted_iota(jnp.int32, (256, 256), 1)
    wanted = jnp.where(place < 128, 2 * place, 2 * (place - 128) + 1)
    select = (source == wanted).astype(F32).astype(BF)
    loads[0].wait()
    for half in range(2):
        block = field_ref[:, :, half * 256:(half + 1) * 256].reshape(CHAN * ROWS, 256)
        both = jnp.dot(block, select, preferred_element_type=F32)
        for c in range(CHAN):
            rows = both[c * ROWS:(c + 1) * ROWS]
            g_ref[half, c * PITCH:c * PITCH + ROWS, :] = rows[:, :128]
            g_ref[2 + half, c * PITCH:c * PITCH + ROWS, :] = rows[:, 128:]
    g_ref[:, CHAN * PITCH:CPAD * PITCH, :] = jnp.zeros((4, (CPAD - CHAN) * PITCH, 128), F32)

    lane = lax.broadcasted_iota(jnp.int32, (CPAD, 128), 1)

    def spread(y, carry):
        first, last = carry
        quarter = [g_ref[n, pl.ds(y, CPAD, stride=PITCH), :] for n in range(4)]
        even = jnp.concatenate(quarter[:2], axis=1)
        odd = jnp.concatenate(quarter[2:], axis=1)
        base = pl.multiple_of((y + 1) * SLAB, SLAB)
        sl_ref[pl.ds(base, CPAD), :] = pltpu.roll(odd, 1, 1).astype(BF)
        sl_ref[pl.ds(base + CPAD, CPAD), :] = even.astype(BF)
        sl_ref[pl.ds(base + 2 * CPAD, CPAD), :] = odd.astype(BF)
        sl_ref[pl.ds(base + 3 * CPAD, CPAD), :] = pltpu.roll(even, 255, 1).astype(BF)
        first = jnp.where(lane == y, pltpu.roll(even[:, :128], y, 1), first)
        last = jnp.where(lane == y, pltpu.roll(odd[:, 128:], y + 1, 1), last)
        return first, last

    empty = jnp.zeros((CPAD, 128), F32)
    first, last = lax.fori_loop(0, ROWS, spread, (empty, empty), unroll=2)
    cols_ref[0] = first.astype(BF)
    cols_ref[1] = last.astype(BF)
    pl.semaphore_wait(barrier, len(around))
    routes = [
        (cols_ref.at[1], colr_ref.at[0], (lat, right)),
        (cols_ref.at[0], colr_ref.at[1], (lat, left)),
        (cols_ref.at[1], colr_ref.at[2], (down, right)),
        (cols_ref.at[0], colr_ref.at[3], (down, left)),
        (cols_ref.at[1], colr_ref.at[4], (up, right)),
        (cols_ref.at[0], colr_ref.at[5], (up, left)),
        (sl_ref.at[pl.ds(ROWS * SLAB + CPAD, 2 * CPAD)], rowr_ref.at[0], (down, lon)),
        (sl_ref.at[pl.ds(SLAB + CPAD, 2 * CPAD)], rowr_ref.at[1], (up, lon)),
    ]
    copies = [
        remote(src, dst, edge_send.at[i], edge_recv.at[i], target)
        for i, (src, dst, target) in enumerate(routes)
    ]
    for i in (6, 7, 0, 1, 2, 3, 4, 5):
        copies[i].start()

    for load in loads[1:]:
        load.wait()
    for n in range(4):
        g_ref[n, 0:16 * CHAN, :] = sw_ref[:, n * 128:(n + 1) * 128].astype(F32)
        for q in range(16):
            part = g_ref[n, pl.ds(q * CHAN, CHAN), :]
            part = jnp.concatenate([part, jnp.zeros((CPAD - CHAN, 128), F32)], axis=0)
            wp_ref[pl.ds(q * CPAD, CPAD), n * 128:(n + 1) * 128] = part.astype(BF)
    for n, ref in enumerate((bias_ref, gain_ref)):
        affine_ref[n] = jnp.broadcast_to(ref[...], (128, D)).T
    for q in range(5):
        wt_ref[:, pl.ds(q * 256, 256)] = wp_ref[pl.ds(q * 256, 256), :].T
    wvt_ref[...] = kvw_ref[:, D:].T
    latents = latents_ref[...]
    centred = latents - jnp.mean(latents, axis=-1, keepdims=True)
    variance = jnp.mean(centred * centred, axis=-1, keepdims=True)
    normed = (centred / jnp.sqrt(variance + 1e-05) * lgain_ref[...]).astype(BF)
    query = jnp.dot(normed, qw_ref[...], preferred_element_type=F32).astype(BF)
    turned = query.T
    for h in range(HEADS):
        mine = (h % 2) * HD
        qt_ref[h, mine:mine + HD, :] = turned[h * HD:(h + 1) * HD, :]
        qt_ref[h, HD - mine:2 * HD - mine, :] = jnp.zeros((HD, LAT), BF)

    for copy in copies:
        copy.wait()

    def patch(y, left_column, right_column, left_roll, right_roll, base):
        a = sl_ref[pl.ds(base, CPAD), 0:128].astype(F32)
        b = sl_ref[pl.ds(base + 3 * CPAD, CPAD), 128:256].astype(F32)
        low = pltpu.roll(left_column.astype(F32), left_roll, 1)
        high = pltpu.roll(right_column.astype(F32), right_roll, 1)
        sl_ref[pl.ds(base, CPAD), 0:128] = jnp.where(lane == 0, low, a).astype(BF)
        sl_ref[pl.ds(base + 3 * CPAD, CPAD), 128:256] = jnp.where(lane == 127, high, b).astype(BF)

    def mend(y, carry):
        base = pl.multiple_of((y + 1) * SLAB, SLAB)
        patch(y, colr_ref[0], colr_ref[1], lax.rem(128 - y, 128), 127 - y, base)
        return carry

    lax.fori_loop(0, ROWS, mend, 0, unroll=4)
    for index, (slab, y, inside) in enumerate([(0, ROWS - 1, lat > 0), (ROWS + 1, 0, lat < NLATD - 1)]):
        base = slab * SLAB
        keep = jnp.where(inside, 1.0, 0.0).astype(F32)
        even = rowr_ref[index, 0:CPAD, :].astype(F32) * keep
        odd = rowr_ref[index, CPAD:2 * CPAD, :].astype(F32) * keep
        sl_ref[pl.ds(base, CPAD), :] = pltpu.roll(odd, 1, 1).astype(BF)
        sl_ref[pl.ds(base + CPAD, CPAD), :] = even.astype(BF)
        sl_ref[pl.ds(base + 2 * CPAD, CPAD), :] = odd.astype(BF)
        sl_ref[pl.ds(base + 3 * CPAD, CPAD), :] = pltpu.roll(even, 255, 1).astype(BF)
        patch(
            y, colr_ref[2 + 2 * index].astype(F32) * keep, colr_ref[3 + 2 * index].astype(F32) * keep,
            (128 - y) % 128, 127 - y, base,
        )

    def stem(r, slot):
        window = sl_ref[pl.ds(pl.multiple_of(r * 2 * SLAB, 2 * SLAB), 4 * SLAB), :]
        stem_ref[slot] = jnp.dot(wt_ref[...], window, preferred_element_type=F32)

    def finish(r, slot):
        wide = lambda n: jnp.concatenate([affine_ref[n]] * 2, axis=1)
        value = stem_ref[slot] + wide(0)
        centred = value - jnp.mean(value, axis=0, keepdims=True)
        variance = jnp.mean(centred * centred, axis=0, keepdims=True)
        turned = (centred * (1.0 / jnp.sqrt(variance + 1e-05)) * wide(1)).astype(BF)
        tokens = turned.T
        tok_ref[r] = tokens
        pltpu.make_async_copy(tok_ref.at[r], tok_hbm.at[r], tok_sem.at[r]).start()
        at = pl.ds(pl.multiple_of(r * TW, TW), TW)
        keys = jnp.dot(tokens, kvw_ref[:, 0:D], preferred_element_type=F32).astype(BF)
        for pair in range(HEADS // 2):
            k_ref[pair, at, :] = keys[:, pair * 128:(pair + 1) * 128]
        values = jnp.dot(wvt_ref[...], turned, preferred_element_type=F32).astype(BF)
        for h in range(HEADS):
            vt_ref[h, 0:HD, at] = values[h * HD:(h + 1) * HD, :]
            vt_ref[h, HD:EXT, at] = jnp.ones((EXT - HD, TW), BF)

    stem(0, 0)

    def two(i, carry):
        stem(2 * i + 1, 1)
        finish(2 * i, 0)
        stem(jnp.minimum(2 * i + 2, TH - 1), 0)
        finish(2 * i + 1, 1)
        return carry

    lax.fori_loop(0, TH // 2, two, 0)

    log2e = 1.4426950408889634
    scale = lambda h: hg_ref[h] * (log2e / 8.0)

    def score(h, j):
        at = pl.ds(pl.multiple_of(j * CH, CH), CH)
        s = jnp.dot(k_ref[h // 2, at, :], qt_ref[h], preferred_element_type=F32)
        s_ref[h % 2, at, :] = s
        mx_ref[h % 2] = jnp.maximum(mx_ref[h % 2], jnp.max(s.reshape(CH // 8, 8, LAT), axis=0))

    def weigh(h, j, top):
        at = pl.ds(pl.multiple_of(j * CH, CH), CH)
        p = jnp.exp2(s_ref[h % 2, at, :] * scale(h) - top).astype(BF)
        acc_ref[...] += jnp.dot(vt_ref[h, :, at], p, preferred_element_type=F32)

    def stat_rows(top, total):
        row = lax.broadcasted_iota(jnp.int32, (16, 128), 0)
        high = total.astype(BF).astype(F32)
        out = jnp.zeros((16, 128), F32)
        for n, value in enumerate((top, high, total - high)):
            out = jnp.where(row == 2 * n, value[:, :128], out)
            out = jnp.where(row == 2 * n + 1, value[:, 128:], out)
        return out.astype(BF)

    def merge(buffer, h, count):
        stats = [buffer[h, s, :, 256:384].astype(F32) for s in range(count)]
        tops = [jnp.concatenate([x[0:1], x[1:2]], axis=1) for x in stats]
        totals = [jnp.concatenate([x[2:3] + x[4:5], x[3:4] + x[5:6]], axis=1) for x in stats]
        top = functools.reduce(jnp.maximum, tops)
        total = jnp.zeros((1, 256), F32)
        acc = jnp.zeros((16, 256), F32)
        for s in range(count):
            fold = jnp.exp2(tops[s] - top)
            total = total + totals[s] * fold
            acc = acc + buffer[h, s, :, 0:256].astype(F32) * fold
        return top, total, acc

    def stage1(h, top):
        acc = acc_ref[...]
        total = acc[HD:HD + 1, :]
        stats = [stat_rows(top[:, g * 256:(g + 1) * 256], total[:, g * 256:(g + 1) * 256]) for g in range(2)]
        for p in range(NLOND):
            e, g = p % 4, p // 4
            src1[h, p, :, 0:256] = acc[16 * e:16 * e + 16, g * 256:(g + 1) * 256].astype(BF)
            src1[h, p, :, 256:384] = stats[g]
        dst1[h, 0] = src1[h, lon]
        for s in range(1, NLOND):
            remote(src1.at[h, lax.rem(lon + s, NLOND)], dst1.at[h, s], send1.at[h], recv1.at[h], lon_peer(s)).start()

    def wait(ref, sem):
        pltpu.make_async_copy(ref, ref, sem).wait()

    def stage2(h):
        wait(dst1.at[h, pl.ds(1, NLOND - 1)], recv1.at[h])
        top, total, acc = merge(dst1, h, NLOND)
        stats = stat_rows(top, total)
        src2[h, :, 0:256] = acc.astype(BF)
        src2[h, :, 256:384] = stats
        dst2[h, lat, :, 0:256] = acc.astype(BF)
        dst2[h, lat, :, 256:384] = stats
        for s in range(1, NLATD):
            remote(src2.at[h], dst2.at[h, lat], send2.at[h], recv2.at[h], lat_peer(s)).start()

    e_at = lax.rem(lon, 4) * 16
    g_at = pl.multiple_of(lon // 4 * 256, 256)

    def stage3(h):
        wait(dst2.at[h, pl.ds(1, NLATD - 1)], recv2.at[h])
        top, total, acc = merge(dst2, h, NLATD)
        here = att.at[pl.ds(pl.multiple_of(h * HD + e_at, 16), 16), pl.ds(g_at, 256)]
        here[...] = (acc / total).astype(BF)
        for s in range(1, NLOND):
            remote(here, here, send3.at[h], recv3.at[h], lon_peer(s)).start()

    for h in range(HEADS + 1):
        slot = h % 2
        if h < HEADS:
            mx_ref[slot] = jnp.full((8, LAT), -jnp.inf, F32)
        if h > 0:
            peak = jnp.max(mx_ref[1 - slot], axis=0, keepdims=True) * scale(h - 1)
            top = (peak + jnp.abs(peak) * 2.0**-7).astype(BF).astype(F32)
            acc_ref[...] = jnp.zeros_like(acc_ref)

        def both(j, carry):
            if h < HEADS:
                score(h, j)
            if h > 0:
                weigh(h - 1, j, top)
            return carry

        lax.fori_loop(0, TOK // CH, both, 0)
        if h > 0:
            stage1(h - 1, top)
        if h > 2:
            stage2(h - 3)
        if h > 5:
            stage3(h - 6)
    stage2(6)
    stage3(3)
    stage3(4)
    stage2(7)
    stage3(5)
    stage3(6)
    stage3(7)
    for r in range(TH):
        wait(tok_ref.at[r], tok_sem.at[r])
    for h in range(HEADS):
        wait(att.at[pl.ds(0, 112), pl.ds(0, 256)], recv3.at[h])
        wait(dst1.at[h, pl.ds(1, NLOND - 1)], send1.at[h])
        wait(dst2.at[h, pl.ds(1, NLATD - 1)], send2.at[h])
        wait(att.at[pl.ds(0, 112), pl.ds(0, 256)], send3.at[h])
    out_ref[...] = att[...]


def encode(field, sw, kvw, latents, qw, bias, gain, lgain, hg):
    dma = pltpu.SemaphoreType.DMA
    return pl.pallas_call(
        encode_kernel,
        out_shape=(jax.ShapeDtypeStruct((TH, TW, D), BF), jax.ShapeDtypeStruct((D, LAT), BF)),
        in_specs=[ANY] * 5 + [VM] * 3 + [SM],
        out_specs=(ANY, VM),
        scratch_shapes=[
            pltpu.VMEM((CHAN, ROWS, COLS), BF),
            pltpu.VMEM((16 * CHAN, D), BF),
            pltpu.VMEM((D, 2 * D), BF),
            pltpu.VMEM((LAT, D), F32),
            pltpu.VMEM((D, D), BF),
            pltpu.VMEM(((ROWS + 2) * SLAB, TW), BF),
            pltpu.VMEM((D, 16 * CPAD), BF),
            pltpu.VMEM((D, D), BF),
            pltpu.VMEM((HEADS, 2 * HD, LAT), BF),
            pltpu.VMEM((4, CPAD * PITCH, 128), F32),
            pltpu.VMEM((16 * CPAD, D), BF),
            pltpu.VMEM((2, CPAD, 128), BF),
            pltpu.VMEM((6, CPAD, 128), BF),
            pltpu.VMEM((2, 2 * CPAD, TW), BF),
            pltpu.VMEM((2, D, 128), F32),
            pltpu.VMEM((2, D, TW), F32),
            pltpu.VMEM((TH, TW, D), BF),
            pltpu.VMEM((HEADS // 2, TOK, 128), BF),
            pltpu.VMEM((HEADS, EXT, TOK), BF),
            pltpu.VMEM((2, TOK, LAT), F32),
            pltpu.VMEM((2, 8, LAT), F32),
            pltpu.VMEM((EXT, LAT), F32),
            pltpu.VMEM((HEADS, NLOND, 16, 384), BF),
            pltpu.VMEM((HEADS, NLOND, 16, 384), BF),
            pltpu.VMEM((HEADS, 16, 384), BF),
            pltpu.VMEM((HEADS, NLATD, 16, 384), BF),
            pltpu.VMEM((D, LAT), BF),
            dma((5,)), dma((TH,)), dma((8,)), dma((8,)),
        ] + [dma((HEADS,))] * 6,
        compiler_params=pltpu.CompilerParams(
            collective_id=0, has_side_effects=True, vmem_limit_bytes=62 * 2**20
        ),
        name="encode",
    )(field, sw, kvw, latents, qw, bias, gain, lgain, hg)


def mix_kernel(tok_hbm, att_ref, ow_ref, gain_ref, tok_out, out_ref, sem):
    quarter = TH // 4
    copies = [
        pltpu.make_async_copy(tok_hbm.at[pl.ds(n * quarter, quarter)], tok_out.at[pl.ds(n * quarter, quarter)], sem.at[n])
        for n in range(4)
    ]
    for copy in copies:
        copy.start()
    mixed = lax.dot_general(
        att_ref[...], ow_ref[...], (((0,), (0,)), ((), ())), preferred_element_type=F32
    )
    centred = mixed - jnp.mean(mixed, axis=-1, keepdims=True)
    variance = jnp.mean(centred * centred, axis=-1, keepdims=True)
    out_ref[...] = centred / jnp.sqrt(variance + 1e-05) * gain_ref[...]
    for copy in copies:
        copy.wait()


def mix(tokens, att, ow, gain):
    return pl.pallas_call(
        mix_kernel,
        out_shape=(jax.ShapeDtypeStruct((TH, TW, D), BF), jax.ShapeDtypeStruct((LAT, D), F32)),
        in_specs=[ANY] + [VM] * 3,
        out_specs=(ANY, VM),
        scratch_shapes=[pltpu.SemaphoreType.DMA((4,))],
        compiler_params=pltpu.CompilerParams(vmem_limit_bytes=62 * 2**20),
        name="mix",
    )(tokens, att, ow, gain)


def shards(
    field, stem_weight, stem_bias, token_gain, kv_weight, latents, latent_gain,
    query_weight, head_gain, out_weight, out_gain,
):
    row = lambda x: x.reshape(1, D)
    tokens, att = encode(
        field, stem_weight, kv_weight, latents, query_weight, row(stem_bias), row(token_gain), row(latent_gain), head_gain
    )
    return mix(tokens, att, out_weight, row(out_gain))


def solution(mesh):
    return jax.shard_map(
        shards,
        mesh=mesh,
        in_specs=(P(None, "lat", "lon"), P(), P(), P(), P(), P(), P(), P(), P(), P(), P()),
        out_specs=(P("lat", "lon", None), P()),
        check_vma=False,
    )
```

```python
import functools

import jax
import jax.numpy as jnp
from jax import lax
from jax.experimental import pallas as pl
from jax.experimental.pallas import tpu as pltpu
from jax.sharding import PartitionSpec as P

HEADS = 8
HD = 64
LAT = 512
D = 512
CHAN = 69
CPAD = 80
ROWS = 32
COLS = 512
TH = 16
TW = 256
TOK = TH * TW
SLAB = 4 * CPAD
NLATD = 16
NLOND = 8
EXT = 80
CH = 2048
PITCH = 40
MESH = pl.DeviceIdType.MESH
F32 = jnp.float32
BF = jnp.bfloat16
VM = pl.BlockSpec(memory_space=pltpu.VMEM)
SM = pl.BlockSpec(memory_space=pltpu.SMEM)
ANY = pl.BlockSpec(memory_space=pl.ANY)


def remote(src, dst, send, recv, target):
    return pltpu.make_async_remote_copy(
        src_ref=src, dst_ref=dst, send_sem=send, recv_sem=recv, device_id=target, device_id_type=MESH
    )


def encode_kernel(
    field_hbm, sw_hbm, kvw_hbm, latents_hbm, qw_hbm, bias_ref, gain_ref, lgain_ref, hg_ref,
    tok_hbm, out_ref,
    field_ref, sw_ref, kvw_ref, latents_ref, qw_ref,
    sl_ref, wt_ref, wvt_ref, qt_ref, g_ref, wp_ref, cols_ref, colr_ref, rowr_ref,
    affine_ref, stem_ref, turned_ref, tok_ref,
    k_ref, vt_ref, s_ref, mx_ref, acc_ref, src1, dst1, src2, dst2, att,
    in_sem, tok_sem, edge_send, edge_recv, send1, recv1, send2, recv2, send3, recv3,
):
    lat = lax.axis_index("lat")
    lon = lax.axis_index("lon")
    up, down = lax.rem(lat + NLATD - 1, NLATD), lax.rem(lat + 1, NLATD)
    left, right = lax.rem(lon + NLOND - 1, NLOND), lax.rem(lon + 1, NLOND)
    loads = [
        pltpu.make_async_copy(src, dst, in_sem.at[i])
        for i, (src, dst) in enumerate([
            (field_hbm, field_ref), (sw_hbm, sw_ref), (kvw_hbm, kvw_ref), (latents_hbm, latents_ref), (qw_hbm, qw_ref),
        ])
    ]
    for load in loads:
        load.start()
    lon_peer = lambda s: (lat, lax.rem(lon + s, NLOND))
    lat_peer = lambda s: (lax.rem(lat + s, NLATD), lon)
    barrier = pltpu.get_barrier_semaphore()
    around = [(up, left), (up, right), (down, left), (down, right)]
    around += [lon_peer(s) for s in range(1, NLOND)] + [lat_peer(s) for s in range(1, NLATD)]
    for target in around:
        pl.semaphore_signal(barrier, inc=1, device_id=target, device_id_type=MESH)

    source = lax.broadcasted_iota(jnp.int32, (256, 256), 0)
    place = lax.broadcasted_iota(jnp.int32, (256, 256), 1)
    wanted = jnp.where(place < 128, 2 * place, 2 * (place - 128) + 1)
    select = (source == wanted).astype(F32).astype(BF)
    loads[0].wait()
    for half in range(2):
        block = field_ref[:, :, half * 256:(half + 1) * 256].reshape(CHAN * ROWS, 256)
        both = jnp.dot(block, select, preferred_element_type=F32)
        for c in range(CHAN):
            rows = both[c * ROWS:(c + 1) * ROWS]
            g_ref[half, c * PITCH:c * PITCH + ROWS, :] = rows[:, :128]
            g_ref[2 + half, c * PITCH:c * PITCH + ROWS, :] = rows[:, 128:]
    g_ref[:, CHAN * PITCH:CPAD * PITCH, :] = jnp.zeros((4, (CPAD - CHAN) * PITCH, 128), F32)

    lane = lax.broadcasted_iota(jnp.int32, (CPAD, 128), 1)

    def spread(y, carry):
        first, last = carry
        quarter = [g_ref[n, pl.ds(y, CPAD, stride=PITCH), :] for n in range(4)]
        even = jnp.concatenate(quarter[:2], axis=1)
        odd = jnp.concatenate(quarter[2:], axis=1)
        base = pl.multiple_of((y + 1) * SLAB, SLAB)
        sl_ref[pl.ds(base, CPAD), :] = pltpu.roll(odd, 1, 1).astype(BF)
        sl_ref[pl.ds(base + CPAD, CPAD), :] = even.astype(BF)
        sl_ref[pl.ds(base + 2 * CPAD, CPAD), :] = odd.astype(BF)
        sl_ref[pl.ds(base + 3 * CPAD, CPAD), :] = pltpu.roll(even, 255, 1).astype(BF)
        first = jnp.where(lane == y, pltpu.roll(even[:, :128], y, 1), first)
        last = jnp.where(lane == y, pltpu.roll(odd[:, 128:], y + 1, 1), last)
        return first, last

    empty = jnp.zeros((CPAD, 128), F32)
    first, last = lax.fori_loop(0, ROWS, spread, (empty, empty), unroll=2)
    cols_ref[0] = first.astype(BF)
    cols_ref[1] = last.astype(BF)
    pl.semaphore_wait(barrier, len(around))
    routes = [
        (cols_ref.at[1], colr_ref.at[0], (lat, right)),
        (cols_ref.at[0], colr_ref.at[1], (lat, left)),
        (cols_ref.at[1], colr_ref.at[2], (down, right)),
        (cols_ref.at[0], colr_ref.at[3], (down, left)),
        (cols_ref.at[1], colr_ref.at[4], (up, right)),
        (cols_ref.at[0], colr_ref.at[5], (up, left)),
        (sl_ref.at[pl.ds(ROWS * SLAB + CPAD, 2 * CPAD)], rowr_ref.at[0], (down, lon)),
        (sl_ref.at[pl.ds(SLAB + CPAD, 2 * CPAD)], rowr_ref.at[1], (up, lon)),
    ]
    copies = [
        remote(src, dst, edge_send.at[i], edge_recv.at[i], target)
        for i, (src, dst, target) in enumerate(routes)
    ]
    for i in (0, 1, 6, 7, 2, 3, 4, 5):
        copies[i].start()

    for load in loads[1:]:
        load.wait()
    for n in range(4):
        g_ref[n, 0:16 * CHAN, :] = sw_ref[:, n * 128:(n + 1) * 128].astype(F32)
        for q in range(16):
            part = g_ref[n, pl.ds(q * CHAN, CHAN), :]
            part = jnp.concatenate([part, jnp.zeros((CPAD - CHAN, 128), F32)], axis=0)
            wp_ref[pl.ds(q * CPAD, CPAD), n * 128:(n + 1) * 128] = part.astype(BF)
    for n, ref in enumerate((bias_ref, gain_ref)):
        affine_ref[n] = jnp.broadcast_to(ref[...], (128, D)).T
    for q in range(5):
        wt_ref[:, pl.ds(q * 256, 256)] = wp_ref[pl.ds(q * 256, 256), :].T
    wvt_ref[...] = kvw_ref[:, D:].T
    latents = latents_ref[...]
    centred = latents - jnp.mean(latents, axis=-1, keepdims=True)
    variance = jnp.mean(centred * centred, axis=-1, keepdims=True)
    normed = (centred / jnp.sqrt(variance + 1e-05) * lgain_ref[...]).astype(BF)
    query = jnp.dot(normed, qw_ref[...], preferred_element_type=F32).astype(BF)
    turned = query.T
    for h in range(HEADS):
        mine = (h % 2) * HD
        qt_ref[h, mine:mine + HD, :] = turned[h * HD:(h + 1) * HD, :]
        qt_ref[h, HD - mine:2 * HD - mine, :] = jnp.zeros((HD, LAT), BF)

    for copy in copies[:2]:
        copy.wait()

    def patch(y, left_column, right_column, left_roll, right_roll, base):
        a = sl_ref[pl.ds(base, CPAD), 0:128].astype(F32)
        b = sl_ref[pl.ds(base + 3 * CPAD, CPAD), 128:256].astype(F32)
        low = pltpu.roll(left_column.astype(F32), left_roll, 1)
        high = pltpu.roll(right_column.astype(F32), right_roll, 1)
        sl_ref[pl.ds(base, CPAD), 0:128] = jnp.where(lane == 0, low, a).astype(BF)
        sl_ref[pl.ds(base + 3 * CPAD, CPAD), 128:256] = jnp.where(lane == 127, high, b).astype(BF)

    def mend(y, carry):
        base = pl.multiple_of((y + 1) * SLAB, SLAB)
        patch(y, colr_ref[0], colr_ref[1], lax.rem(128 - y, 128), 127 - y, base)
        return carry

    lax.fori_loop(0, ROWS, mend, 0, unroll=4)

    def stem(r, slot):
        window = sl_ref[pl.ds(pl.multiple_of(r * 2 * SLAB, 2 * SLAB), 4 * SLAB), :]
        stem_ref[slot] = jnp.dot(wt_ref[...], window, preferred_element_type=F32)

    def norm(r, slot):
        wide = lambda n: jnp.concatenate([affine_ref[n]] * 2, axis=1)
        value = stem_ref[slot] + wide(0)
        centred = value - jnp.mean(value, axis=0, keepdims=True)
        variance = jnp.mean(centred * centred, axis=0, keepdims=True)
        turned = (centred * (1.0 / jnp.sqrt(variance + 1e-05)) * wide(1)).astype(BF)
        turned_ref[slot] = turned
        tok_ref[r] = turned.T

    def project(r, slot):
        at = pl.ds(pl.multiple_of(r * TW, TW), TW)
        keys = jnp.dot(tok_ref[r], kvw_ref[:, 0:D], preferred_element_type=F32).astype(BF)
        for pair in range(HEADS // 2):
            k_ref[pair, at, :] = keys[:, pair * 128:(pair + 1) * 128]
        values = jnp.dot(wvt_ref[...], turned_ref[slot], preferred_element_type=F32).astype(BF)
        for h in range(HEADS):
            vt_ref[h, 0:HD, at] = values[h * HD:(h + 1) * HD, :]
            vt_ref[h, HD:EXT, at] = jnp.ones((EXT - HD, TW), BF)

    def ship(r):
        pltpu.make_async_copy(tok_ref.at[r], tok_hbm.at[r], tok_sem.at[r]).start()

    def border():
        for copy in copies[2:]:
            copy.wait()
        for index, (slab, y, inside) in enumerate([(0, ROWS - 1, lat > 0), (ROWS + 1, 0, lat < NLATD - 1)]):
            base = slab * SLAB
            keep = jnp.where(inside, 1.0, 0.0).astype(F32)
            even = rowr_ref[index, 0:CPAD, :].astype(F32) * keep
            odd = rowr_ref[index, CPAD:2 * CPAD, :].astype(F32) * keep
            sl_ref[pl.ds(base, CPAD), :] = pltpu.roll(odd, 1, 1).astype(BF)
            sl_ref[pl.ds(base + CPAD, CPAD), :] = even.astype(BF)
            sl_ref[pl.ds(base + 2 * CPAD, CPAD), :] = odd.astype(BF)
            sl_ref[pl.ds(base + 3 * CPAD, CPAD), :] = pltpu.roll(even, 255, 1).astype(BF)
            patch(
                y, colr_ref[2 + 2 * index].astype(F32) * keep, colr_ref[3 + 2 * index].astype(F32) * keep,
                (128 - y) % 128, 127 - y, base,
            )

    stem(1, 1)
    norm(1, 1)
    stem(2, 0)

    def two(i, carry):
        r = 2 * i + 1
        ship(r)
        project(r, 1)
        norm(r + 1, 0)
        stem(r + 2, 1)
        ship(r + 1)
        project(r + 1, 0)
        norm(r + 2, 1)
        stem(r + 3, 0)
        return carry

    lax.fori_loop(0, 6, two, 0)
    border()
    ship(13)
    project(13, 1)
    norm(14, 0)
    stem(15, 1)
    ship(14)
    project(14, 0)
    norm(15, 1)
    stem(0, 0)
    ship(15)
    project(15, 1)
    norm(0, 0)
    ship(0)
    project(0, 0)

    log2e = 1.4426950408889634
    scale = lambda h: hg_ref[h] * (log2e / 8.0)

    def score(h, j):
        at = pl.ds(pl.multiple_of(j * CH, CH), CH)
        s = jnp.dot(k_ref[h // 2, at, :], qt_ref[h], preferred_element_type=F32)
        s_ref[h % 2, at, :] = s
        mx_ref[h % 2] = jnp.maximum(mx_ref[h % 2], jnp.max(s.reshape(CH // 8, 8, LAT), axis=0))

    def weigh(h, j, top):
        at = pl.ds(pl.multiple_of(j * CH, CH), CH)
        p = jnp.exp2(s_ref[h % 2, at, :] * scale(h) - top).astype(BF)
        acc_ref[...] += jnp.dot(vt_ref[h, :, at], p, preferred_element_type=F32)

    def stat_rows(top, total):
        row = lax.broadcasted_iota(jnp.int32, (16, 128), 0)
        high = total.astype(BF).astype(F32)
        out = jnp.zeros((16, 128), F32)
        for n, value in enumerate((top, high, total - high)):
            out = jnp.where(row == 2 * n, value[:, :128], out)
            out = jnp.where(row == 2 * n + 1, value[:, 128:], out)
        return out.astype(BF)

    def merge(buffer, h, count):
        stats = [buffer[h, s, :, 256:384].astype(F32) for s in range(count)]
        tops = [jnp.concatenate([x[0:1], x[1:2]], axis=1) for x in stats]
        totals = [jnp.concatenate([x[2:3] + x[4:5], x[3:4] + x[5:6]], axis=1) for x in stats]
        top = functools.reduce(jnp.maximum, tops)
        total = jnp.zeros((1, 256), F32)
        acc = jnp.zeros((16, 256), F32)
        for s in range(count):
            fold = jnp.exp2(tops[s] - top)
            total = total + totals[s] * fold
            acc = acc + buffer[h, s, :, 0:256].astype(F32) * fold
        return top, total, acc

    def stage1(h, top):
        acc = acc_ref[...]
        total = acc[HD:HD + 1, :]
        stats = [stat_rows(top[:, g * 256:(g + 1) * 256], total[:, g * 256:(g + 1) * 256]) for g in range(2)]
        for p in range(NLOND):
            e, g = p % 4, p // 4
            src1[h, p, :, 0:256] = acc[16 * e:16 * e + 16, g * 256:(g + 1) * 256].astype(BF)
            src1[h, p, :, 256:384] = stats[g]
        dst1[h, 0] = src1[h, lon]
        for s in range(1, NLOND):
            remote(src1.at[h, lax.rem(lon + s, NLOND)], dst1.at[h, s], send1.at[h], recv1.at[h], lon_peer(s)).start()

    def wait(ref, sem):
        pltpu.make_async_copy(ref, ref, sem).wait()

    def stage2(h):
        wait(dst1.at[h, pl.ds(1, NLOND - 1)], recv1.at[h])
        top, total, acc = merge(dst1, h, NLOND)
        stats = stat_rows(top, total)
        src2[h, :, 0:256] = acc.astype(BF)
        src2[h, :, 256:384] = stats
        dst2[h, lat, :, 0:256] = acc.astype(BF)
        dst2[h, lat, :, 256:384] = stats
        for s in range(1, NLATD):
            remote(src2.at[h], dst2.at[h, lat], send2.at[h], recv2.at[h], lat_peer(s)).start()

    e_at = lax.rem(lon, 4) * 16
    g_at = pl.multiple_of(lon // 4 * 256, 256)

    def stage3(h):
        wait(dst2.at[h, pl.ds(1, NLATD - 1)], recv2.at[h])
        top, total, acc = merge(dst2, h, NLATD)
        here = att.at[pl.ds(pl.multiple_of(h * HD + e_at, 16), 16), pl.ds(g_at, 256)]
        here[...] = (acc / total).astype(BF)
        for s in range(1, NLOND):
            remote(here, here, send3.at[h], recv3.at[h], lon_peer(s)).start()

    for h in range(HEADS + 1):
        slot = h % 2
        if h < HEADS:
            mx_ref[slot] = jnp.full((8, LAT), -jnp.inf, F32)
        if h > 0:
            peak = jnp.max(mx_ref[1 - slot], axis=0, keepdims=True) * scale(h - 1)
            top = (peak + jnp.abs(peak) * 2.0**-7).astype(BF).astype(F32)
            acc_ref[...] = jnp.zeros_like(acc_ref)

        def both(j, carry):
            if h < HEADS:
                score(h, j)
            if h > 0:
                weigh(h - 1, j, top)
            return carry

        lax.fori_loop(0, TOK // CH, both, 0)
        if h > 0:
            stage1(h - 1, top)
        if h > 2:
            stage2(h - 3)
        if h > 5:
            stage3(h - 6)
    stage2(6)
    stage3(3)
    stage3(4)
    stage2(7)
    stage3(5)
    stage3(6)
    stage3(7)
    for r in range(TH):
        wait(tok_ref.at[r], tok_sem.at[r])
    for h in range(HEADS):
        wait(att.at[pl.ds(0, 112), pl.ds(0, 256)], recv3.at[h])
        wait(dst1.at[h, pl.ds(1, NLOND - 1)], send1.at[h])
        wait(dst2.at[h, pl.ds(1, NLATD - 1)], send2.at[h])
        wait(att.at[pl.ds(0, 112), pl.ds(0, 256)], send3.at[h])
    out_ref[...] = att[...]


def encode(field, sw, kvw, latents, qw, bias, gain, lgain, hg):
    dma = pltpu.SemaphoreType.DMA
    return pl.pallas_call(
        encode_kernel,
        out_shape=(jax.ShapeDtypeStruct((TH, TW, D), BF), jax.ShapeDtypeStruct((D, LAT), BF)),
        in_specs=[ANY] * 5 + [VM] * 3 + [SM],
        out_specs=(ANY, VM),
        scratch_shapes=[
            pltpu.VMEM((CHAN, ROWS, COLS), BF),
            pltpu.VMEM((16 * CHAN, D), BF),
            pltpu.VMEM((D, 2 * D), BF),
            pltpu.VMEM((LAT, D), F32),
            pltpu.VMEM((D, D), BF),
            pltpu.VMEM(((ROWS + 2) * SLAB, TW), BF),
            pltpu.VMEM((D, 16 * CPAD), BF),
            pltpu.VMEM((D, D), BF),
            pltpu.VMEM((HEADS, 2 * HD, LAT), BF),
            pltpu.VMEM((4, CPAD * PITCH, 128), F32),
            pltpu.VMEM((16 * CPAD, D), BF),
            pltpu.VMEM((2, CPAD, 128), BF),
            pltpu.VMEM((6, CPAD, 128), BF),
            pltpu.VMEM((2, 2 * CPAD, TW), BF),
            pltpu.VMEM((2, D, 128), F32),
            pltpu.VMEM((2, D, TW), F32),
            pltpu.VMEM((2, D, TW), BF),
            pltpu.VMEM((TH, TW, D), BF),
            pltpu.VMEM((HEADS // 2, TOK, 128), BF),
            pltpu.VMEM((HEADS, EXT, TOK), BF),
            pltpu.VMEM((2, TOK, LAT), F32),
            pltpu.VMEM((2, 8, LAT), F32),
            pltpu.VMEM((EXT, LAT), F32),
            pltpu.VMEM((HEADS, NLOND, 16, 384), BF),
            pltpu.VMEM((HEADS, NLOND, 16, 384), BF),
            pltpu.VMEM((HEADS, 16, 384), BF),
            pltpu.VMEM((HEADS, NLATD, 16, 384), BF),
            pltpu.VMEM((D, LAT), BF),
            dma((5,)), dma((TH,)), dma((8,)), dma((8,)),
        ] + [dma((HEADS,))] * 6,
        compiler_params=pltpu.CompilerParams(
            collective_id=0, has_side_effects=True, vmem_limit_bytes=62 * 2**20
        ),
        name="encode",
    )(field, sw, kvw, latents, qw, bias, gain, lgain, hg)


def mix_kernel(tok_hbm, att_ref, ow_ref, gain_ref, tok_out, out_ref, hold, in_sem, out_sem):
    ins = [pltpu.make_async_copy(tok_hbm.at[pl.ds(2 * n, 2)], hold.at[pl.ds(2 * n, 2)], in_sem.at[n]) for n in range(TH // 2)]
    outs = [pltpu.make_async_copy(hold.at[pl.ds(2 * n, 2)], tok_out.at[pl.ds(2 * n, 2)], out_sem.at[n]) for n in range(TH // 2)]
    for copy in ins:
        copy.start()
    weight = ow_ref[...]
    for n in range(4):
        for m in (2 * n, 2 * n + 1):
            ins[m].wait()
            outs[m].start()
        mixed = lax.dot_general(
            att_ref[:, n * 128:(n + 1) * 128], weight, (((0,), (0,)), ((), ())), preferred_element_type=F32
        )
        centred = mixed - jnp.mean(mixed, axis=-1, keepdims=True)
        variance = jnp.mean(centred * centred, axis=-1, keepdims=True)
        out_ref[n * 128:(n + 1) * 128, :] = centred / jnp.sqrt(variance + 1e-05) * gain_ref[...]
    for copy in outs:
        copy.wait()


def mix(tokens, att, ow, gain):
    return pl.pallas_call(
        mix_kernel,
        out_shape=(jax.ShapeDtypeStruct((TH, TW, D), BF), jax.ShapeDtypeStruct((LAT, D), F32)),
        in_specs=[ANY] + [VM] * 3,
        out_specs=(ANY, VM),
        scratch_shapes=[pltpu.VMEM((TH, TW, D), BF)] + [pltpu.SemaphoreType.DMA((TH // 2,))] * 2,
        compiler_params=pltpu.CompilerParams(vmem_limit_bytes=62 * 2**20),
        name="mix",
    )(tokens, att, ow, gain)


def shards(
    field, stem_weight, stem_bias, token_gain, kv_weight, latents, latent_gain,
    query_weight, head_gain, out_weight, out_gain,
):
    row = lambda x: x.reshape(1, D)
    tokens, att = encode(
        field, stem_weight, kv_weight, latents, query_weight, row(stem_bias), row(token_gain), row(latent_gain), head_gain
    )
    return mix(tokens, att, out_weight, row(out_gain))


def solution(mesh):
    return jax.shard_map(
        shards,
        mesh=mesh,
        in_specs=(P(None, "lat", "lon"), P(), P(), P(), P(), P(), P(), P(), P(), P(), P()),
        out_specs=(P("lat", "lon", None), P()),
        check_vma=False,
    )
```

```python
import functools

import jax
import jax.numpy as jnp
from jax import lax
from jax.experimental import pallas as pl
from jax.experimental.pallas import tpu as pltpu
from jax.sharding import PartitionSpec as P

HEADS = 8
HD = 64
LAT = 512
D = 512
CHAN = 69
CPAD = 80
ROWS = 32
COLS = 512
TH = 16
TW = 256
TOK = TH * TW
SLAB = 4 * CPAD
NLATD = 16
NLOND = 8
EXT = 80
CH = 2048
PITCH = 40
LIMIT = 58
MESH = pl.DeviceIdType.MESH
F32 = jnp.float32
BF = jnp.bfloat16
VM = pl.BlockSpec(memory_space=pltpu.VMEM)
SM = pl.BlockSpec(memory_space=pltpu.SMEM)
ANY = pl.BlockSpec(memory_space=pl.ANY)


def remote(src, dst, send, recv, target):
    return pltpu.make_async_remote_copy(
        src_ref=src, dst_ref=dst, send_sem=send, recv_sem=recv, device_id=target, device_id_type=MESH
    )


def encode_kernel(
    field_hbm, sw_hbm, kvw_hbm, latents_hbm, qw_hbm, bias_ref, gain_ref, lgain_ref, hg_ref,
    tok_ref, out_ref,
    field_ref, sw_ref, kvw_ref, latents_ref, qw_ref,
    sl_ref, wt_ref, wvt_ref, qt_ref, g_ref, wp_ref, cols_ref, colr_ref, rowr_ref,
    affine_ref, stem_ref, turned_ref,
    k_ref, vt_ref, s_ref, mx_ref, acc_ref, src1, dst1, src2, dst2, att,
    in_sem, edge_send, edge_recv, send1, recv1, send2, recv2, send3, recv3,
):
    lat = lax.axis_index("lat")
    lon = lax.axis_index("lon")
    up, down = lax.rem(lat + NLATD - 1, NLATD), lax.rem(lat + 1, NLATD)
    left, right = lax.rem(lon + NLOND - 1, NLOND), lax.rem(lon + 1, NLOND)
    loads = [
        pltpu.make_async_copy(src, dst, in_sem.at[i])
        for i, (src, dst) in enumerate([
            (field_hbm, field_ref), (sw_hbm, sw_ref), (kvw_hbm, kvw_ref), (latents_hbm, latents_ref), (qw_hbm, qw_ref),
        ])
    ]
    for load in loads:
        load.start()
    lon_peer = lambda s: (lat, lax.rem(lon + s, NLOND))
    lat_peer = lambda s: (lax.rem(lat + s, NLATD), lon)
    barrier = pltpu.get_barrier_semaphore()
    around = [(up, left), (up, right), (down, left), (down, right)]
    around += [lon_peer(s) for s in range(1, NLOND)] + [lat_peer(s) for s in range(1, NLATD)]
    for target in around:
        pl.semaphore_signal(barrier, inc=1, device_id=target, device_id_type=MESH)

    source = lax.broadcasted_iota(jnp.int32, (256, 256), 0)
    place = lax.broadcasted_iota(jnp.int32, (256, 256), 1)
    wanted = jnp.where(place < 128, 2 * place, 2 * (place - 128) + 1)
    select = (source == wanted).astype(F32).astype(BF)
    loads[0].wait()
    for half in range(2):
        block = field_ref[:, :, half * 256:(half + 1) * 256].reshape(CHAN * ROWS, 256)
        both = jnp.dot(block, select, preferred_element_type=F32)
        for c in range(CHAN):
            rows = both[c * ROWS:(c + 1) * ROWS]
            g_ref[half, c * PITCH:c * PITCH + ROWS, :] = rows[:, :128]
            g_ref[2 + half, c * PITCH:c * PITCH + ROWS, :] = rows[:, 128:]
    g_ref[:, CHAN * PITCH:CPAD * PITCH, :] = jnp.zeros((4, (CPAD - CHAN) * PITCH, 128), F32)

    lane = lax.broadcasted_iota(jnp.int32, (CPAD, 128), 1)

    def spread(y, carry):
        first, last = carry
        quarter = [g_ref[n, pl.ds(y, CPAD, stride=PITCH), :] for n in range(4)]
        even = jnp.concatenate(quarter[:2], axis=1)
        odd = jnp.concatenate(quarter[2:], axis=1)
        base = pl.multiple_of((y + 1) * SLAB, SLAB)
        sl_ref[pl.ds(base, CPAD), :] = pltpu.roll(odd, 1, 1).astype(BF)
        sl_ref[pl.ds(base + CPAD, CPAD), :] = even.astype(BF)
        sl_ref[pl.ds(base + 2 * CPAD, CPAD), :] = odd.astype(BF)
        sl_ref[pl.ds(base + 3 * CPAD, CPAD), :] = pltpu.roll(even, 255, 1).astype(BF)
        first = jnp.where(lane == y, pltpu.roll(even[:, :128], y, 1), first)
        last = jnp.where(lane == y, pltpu.roll(odd[:, 128:], y + 1, 1), last)
        return first, last

    empty = jnp.zeros((CPAD, 128), F32)
    first, last = lax.fori_loop(0, ROWS, spread, (empty, empty), unroll=2)
    cols_ref[0] = first.astype(BF)
    cols_ref[1] = last.astype(BF)
    pl.semaphore_wait(barrier, len(around))
    routes = [
        (cols_ref.at[1], colr_ref.at[0], (lat, right)),
        (cols_ref.at[0], colr_ref.at[1], (lat, left)),
        (cols_ref.at[1], colr_ref.at[2], (down, right)),
        (cols_ref.at[0], colr_ref.at[3], (down, left)),
        (cols_ref.at[1], colr_ref.at[4], (up, right)),
        (cols_ref.at[0], colr_ref.at[5], (up, left)),
        (sl_ref.at[pl.ds(ROWS * SLAB + CPAD, 2 * CPAD)], rowr_ref.at[0], (down, lon)),
        (sl_ref.at[pl.ds(SLAB + CPAD, 2 * CPAD)], rowr_ref.at[1], (up, lon)),
    ]
    copies = [
        remote(src, dst, edge_send.at[i], edge_recv.at[i], target)
        for i, (src, dst, target) in enumerate(routes)
    ]
    for i in (0, 1, 6, 7, 2, 3, 4, 5):
        copies[i].start()

    for load in loads[1:]:
        load.wait()
    for n in range(4):
        g_ref[n, 0:16 * CHAN, :] = sw_ref[:, n * 128:(n + 1) * 128].astype(F32)
        for q in range(16):
            part = g_ref[n, pl.ds(q * CHAN, CHAN), :]
            part = jnp.concatenate([part, jnp.zeros((CPAD - CHAN, 128), F32)], axis=0)
            wp_ref[pl.ds(q * CPAD, CPAD), n * 128:(n + 1) * 128] = part.astype(BF)
    for n, ref in enumerate((bias_ref, gain_ref)):
        affine_ref[n] = jnp.broadcast_to(ref[...], (128, D)).T
    for q in range(5):
        wt_ref[:, pl.ds(q * 256, 256)] = wp_ref[pl.ds(q * 256, 256), :].T
    wvt_ref[...] = kvw_ref[:, D:].T
    latents = latents_ref[...]
    centred = latents - jnp.mean(latents, axis=-1, keepdims=True)
    variance = jnp.mean(centred * centred, axis=-1, keepdims=True)
    normed = (centred / jnp.sqrt(variance + 1e-05) * lgain_ref[...]).astype(BF)
    query = jnp.dot(normed, qw_ref[...], preferred_element_type=F32).astype(BF)
    turned = query.T
    for h in range(HEADS):
        mine = (h % 2) * HD
        qt_ref[h, mine:mine + HD, :] = turned[h * HD:(h + 1) * HD, :]
        qt_ref[h, HD - mine:2 * HD - mine, :] = jnp.zeros((HD, LAT), BF)

    for copy in copies[:2]:
        copy.wait()

    def patch(y, left_column, right_column, left_roll, right_roll, base):
        a = sl_ref[pl.ds(base, CPAD), 0:128].astype(F32)
        b = sl_ref[pl.ds(base + 3 * CPAD, CPAD), 128:256].astype(F32)
        low = pltpu.roll(left_column.astype(F32), left_roll, 1)
        high = pltpu.roll(right_column.astype(F32), right_roll, 1)
        sl_ref[pl.ds(base, CPAD), 0:128] = jnp.where(lane == 0, low, a).astype(BF)
        sl_ref[pl.ds(base + 3 * CPAD, CPAD), 128:256] = jnp.where(lane == 127, high, b).astype(BF)

    def mend(y, carry):
        base = pl.multiple_of((y + 1) * SLAB, SLAB)
        patch(y, colr_ref[0], colr_ref[1], lax.rem(128 - y, 128), 127 - y, base)
        return carry

    lax.fori_loop(0, ROWS, mend, 0, unroll=4)

    def stem(r, slot):
        window = sl_ref[pl.ds(pl.multiple_of(r * 2 * SLAB, 2 * SLAB), 4 * SLAB), :]
        stem_ref[slot] = jnp.dot(wt_ref[...], window, preferred_element_type=F32)

    def norm(r, slot):
        wide = lambda n: jnp.concatenate([affine_ref[n]] * 2, axis=1)
        value = stem_ref[slot] + wide(0)
        centred = value - jnp.mean(value, axis=0, keepdims=True)
        variance = jnp.mean(centred * centred, axis=0, keepdims=True)
        turned = (centred * (1.0 / jnp.sqrt(variance + 1e-05)) * wide(1)).astype(BF)
        turned_ref[slot] = turned
        tok_ref[r] = turned.T

    def project(r, slot):
        at = pl.ds(pl.multiple_of(r * TW, TW), TW)
        keys = jnp.dot(tok_ref[r], kvw_ref[:, 0:D], preferred_element_type=F32).astype(BF)
        for pair in range(HEADS // 2):
            k_ref[pair, at, :] = keys[:, pair * 128:(pair + 1) * 128]
        values = jnp.dot(wvt_ref[...], turned_ref[slot], preferred_element_type=F32).astype(BF)
        for h in range(HEADS):
            vt_ref[h, 0:HD, at] = values[h * HD:(h + 1) * HD, :]
            vt_ref[h, HD:EXT, at] = jnp.ones((EXT - HD, TW), BF)

    def border():
        for copy in copies[2:]:
            copy.wait()
        for index, (slab, y, inside) in enumerate([(0, ROWS - 1, lat > 0), (ROWS + 1, 0, lat < NLATD - 1)]):
            base = slab * SLAB
            keep = jnp.where(inside, 1.0, 0.0).astype(F32)
            even = rowr_ref[index, 0:CPAD, :].astype(F32) * keep
            odd = rowr_ref[index, CPAD:2 * CPAD, :].astype(F32) * keep
            sl_ref[pl.ds(base, CPAD), :] = pltpu.roll(odd, 1, 1).astype(BF)
            sl_ref[pl.ds(base + CPAD, CPAD), :] = even.astype(BF)
            sl_ref[pl.ds(base + 2 * CPAD, CPAD), :] = odd.astype(BF)
            sl_ref[pl.ds(base + 3 * CPAD, CPAD), :] = pltpu.roll(even, 255, 1).astype(BF)
            patch(
                y, colr_ref[2 + 2 * index].astype(F32) * keep, colr_ref[3 + 2 * index].astype(F32) * keep,
                (128 - y) % 128, 127 - y, base,
            )

    stem(1, 1)
    norm(1, 1)
    stem(2, 0)

    def two(i, carry):
        r = 2 * i + 1
        project(r, 1)
        norm(r + 1, 0)
        stem(r + 2, 1)
        project(r + 1, 0)
        norm(r + 2, 1)
        stem(r + 3, 0)
        return carry

    lax.fori_loop(0, 6, two, 0)
    border()
    project(13, 1)
    norm(14, 0)
    stem(15, 1)
    project(14, 0)
    norm(15, 1)
    stem(0, 0)
    project(15, 1)
    norm(0, 0)
    project(0, 0)

    log2e = 1.4426950408889634
    scale = lambda h: hg_ref[h] * (log2e / 8.0)

    def score(h, j):
        at = pl.ds(pl.multiple_of(j * CH, CH), CH)
        s = jnp.dot(k_ref[h // 2, at, :], qt_ref[h], preferred_element_type=F32)
        s_ref[h % 2, at, :] = s
        mx_ref[h % 2] = jnp.maximum(mx_ref[h % 2], jnp.max(s.reshape(CH // 8, 8, LAT), axis=0))

    def weigh(h, j, top):
        at = pl.ds(pl.multiple_of(j * CH, CH), CH)
        p = jnp.exp2(s_ref[h % 2, at, :] * scale(h) - top).astype(BF)
        acc_ref[...] += jnp.dot(vt_ref[h, :, at], p, preferred_element_type=F32)

    def stat_rows(top, total):
        row = lax.broadcasted_iota(jnp.int32, (16, 128), 0)
        high = total.astype(BF).astype(F32)
        out = jnp.zeros((16, 128), F32)
        for n, value in enumerate((top, high, total - high)):
            out = jnp.where(row == 2 * n, value[:, :128], out)
            out = jnp.where(row == 2 * n + 1, value[:, 128:], out)
        return out.astype(BF)

    def merge(buffer, h, count):
        stats = [buffer[h, s, :, 256:384].astype(F32) for s in range(count)]
        tops = [jnp.concatenate([x[0:1], x[1:2]], axis=1) for x in stats]
        totals = [jnp.concatenate([x[2:3] + x[4:5], x[3:4] + x[5:6]], axis=1) for x in stats]
        top = functools.reduce(jnp.maximum, tops)
        total = jnp.zeros((1, 256), F32)
        acc = jnp.zeros((16, 256), F32)
        for s in range(count):
            fold = jnp.exp2(tops[s] - top)
            total = total + totals[s] * fold
            acc = acc + buffer[h, s, :, 0:256].astype(F32) * fold
        return top, total, acc

    def stage1(h, top):
        acc = acc_ref[...]
        total = acc[HD:HD + 1, :]
        stats = [stat_rows(top[:, g * 256:(g + 1) * 256], total[:, g * 256:(g + 1) * 256]) for g in range(2)]
        for p in range(NLOND):
            e, g = p % 4, p // 4
            src1[h, p, :, 0:256] = acc[16 * e:16 * e + 16, g * 256:(g + 1) * 256].astype(BF)
            src1[h, p, :, 256:384] = stats[g]
        dst1[h, 0] = src1[h, lon]
        for s in range(1, NLOND):
            remote(src1.at[h, lax.rem(lon + s, NLOND)], dst1.at[h, s], send1.at[h], recv1.at[h], lon_peer(s)).start()

    def wait(ref, sem):
        pltpu.make_async_copy(ref, ref, sem).wait()

    def stage2(h):
        wait(dst1.at[h, pl.ds(1, NLOND - 1)], recv1.at[h])
        top, total, acc = merge(dst1, h, NLOND)
        stats = stat_rows(top, total)
        src2[h, :, 0:256] = acc.astype(BF)
        src2[h, :, 256:384] = stats
        dst2[h, lat, :, 0:256] = acc.astype(BF)
        dst2[h, lat, :, 256:384] = stats
        for s in range(1, NLATD):
            remote(src2.at[h], dst2.at[h, lat], send2.at[h], recv2.at[h], lat_peer(s)).start()

    e_at = lax.rem(lon, 4) * 16
    g_at = pl.multiple_of(lon // 4 * 256, 256)

    def stage3(h):
        wait(dst2.at[h, pl.ds(1, NLATD - 1)], recv2.at[h])
        top, total, acc = merge(dst2, h, NLATD)
        here = att.at[pl.ds(pl.multiple_of(h * HD + e_at, 16), 16), pl.ds(g_at, 256)]
        here[...] = (acc / total).astype(BF)
        for s in range(1, NLOND):
            remote(here, here, send3.at[h], recv3.at[h], lon_peer(s)).start()

    for h in range(HEADS + 1):
        slot = h % 2
        if h < HEADS:
            mx_ref[slot] = jnp.full((8, LAT), -jnp.inf, F32)
        if h > 0:
            peak = jnp.max(mx_ref[1 - slot], axis=0, keepdims=True) * scale(h - 1)
            top = (peak + jnp.abs(peak) * 2.0**-7).astype(BF).astype(F32)
            acc_ref[...] = jnp.zeros_like(acc_ref)

        def both(j, carry):
            if h < HEADS:
                score(h, j)
            if h > 0:
                weigh(h - 1, j, top)
            return carry

        lax.fori_loop(0, TOK // CH, both, 0)
        if h > 0:
            stage1(h - 1, top)
        if h > 2:
            stage2(h - 3)
        if h > 5:
            stage3(h - 6)
    stage2(6)
    stage3(3)
    stage3(4)
    stage2(7)
    stage3(5)
    stage3(6)
    stage3(7)
    for h in range(HEADS):
        wait(att.at[pl.ds(0, 112), pl.ds(0, 256)], recv3.at[h])
        wait(dst1.at[h, pl.ds(1, NLOND - 1)], send1.at[h])
        wait(dst2.at[h, pl.ds(1, NLATD - 1)], send2.at[h])
        wait(att.at[pl.ds(0, 112), pl.ds(0, 256)], send3.at[h])
    out_ref[...] = att[...]


def encode(field, sw, kvw, latents, qw, bias, gain, lgain, hg):
    dma = pltpu.SemaphoreType.DMA
    return pl.pallas_call(
        encode_kernel,
        out_shape=(pltpu.VMEM((TH, TW, D), BF), pltpu.VMEM((D, LAT), BF)),
        in_specs=[ANY] * 5 + [VM] * 3 + [SM],
        out_specs=(VM, VM),
        scratch_shapes=[
            pltpu.VMEM((CHAN, ROWS, COLS), BF),
            pltpu.VMEM((16 * CHAN, D), BF),
            pltpu.VMEM((D, 2 * D), BF),
            pltpu.VMEM((LAT, D), F32),
            pltpu.VMEM((D, D), BF),
            pltpu.VMEM(((ROWS + 2) * SLAB, TW), BF),
            pltpu.VMEM((D, 16 * CPAD), BF),
            pltpu.VMEM((D, D), BF),
            pltpu.VMEM((HEADS, 2 * HD, LAT), BF),
            pltpu.VMEM((4, CPAD * PITCH, 128), F32),
            pltpu.VMEM((16 * CPAD, D), BF),
            pltpu.VMEM((2, CPAD, 128), BF),
            pltpu.VMEM((6, CPAD, 128), BF),
            pltpu.VMEM((2, 2 * CPAD, TW), BF),
            pltpu.VMEM((2, D, 128), F32),
            pltpu.VMEM((2, D, TW), F32),
            pltpu.VMEM((2, D, TW), BF),
            pltpu.VMEM((HEADS // 2, TOK, 128), BF),
            pltpu.VMEM((HEADS, EXT, TOK), BF),
            pltpu.VMEM((2, TOK, LAT), F32),
            pltpu.VMEM((2, 8, LAT), F32),
            pltpu.VMEM((EXT, LAT), F32),
            pltpu.VMEM((HEADS, NLOND, 16, 384), BF),
            pltpu.VMEM((HEADS, NLOND, 16, 384), BF),
            pltpu.VMEM((HEADS, 16, 384), BF),
            pltpu.VMEM((HEADS, NLATD, 16, 384), BF),
            pltpu.VMEM((D, LAT), BF),
            dma((5,)), dma((8,)), dma((8,)),
        ] + [dma((HEADS,))] * 6,
        compiler_params=pltpu.CompilerParams(
            collective_id=0, has_side_effects=True, vmem_limit_bytes=LIMIT * 2**20
        ),
        name="encode",
    )(field, sw, kvw, latents, qw, bias, gain, lgain, hg)


def mix_kernel(tok_in, att_ref, ow_ref, gain_ref, tok_out, out_ref, sem):
    copies = [pltpu.make_async_copy(tok_in.at[pl.ds(4 * n, 4)], tok_out.at[pl.ds(4 * n, 4)], sem.at[n]) for n in range(4)]
    for copy in copies:
        copy.start()
    weight = ow_ref[...]
    for n in range(4):
        mixed = lax.dot_general(
            att_ref[:, n * 128:(n + 1) * 128], weight, (((0,), (0,)), ((), ())), preferred_element_type=F32
        )
        centred = mixed - jnp.mean(mixed, axis=-1, keepdims=True)
        variance = jnp.mean(centred * centred, axis=-1, keepdims=True)
        out_ref[n * 128:(n + 1) * 128, :] = centred / jnp.sqrt(variance + 1e-05) * gain_ref[...]
    for copy in copies:
        copy.wait()


def mix(tokens, att, ow, gain):
    return pl.pallas_call(
        mix_kernel,
        out_shape=(jax.ShapeDtypeStruct((TH, TW, D), BF), jax.ShapeDtypeStruct((LAT, D), F32)),
        in_specs=[ANY] + [VM] * 3,
        out_specs=(ANY, VM),
        scratch_shapes=[pltpu.SemaphoreType.DMA((4,))],
        compiler_params=pltpu.CompilerParams(vmem_limit_bytes=12 * 2**20),
        name="mix",
    )(tokens, att, ow, gain)


def shards(
    field, stem_weight, stem_bias, token_gain, kv_weight, latents, latent_gain,
    query_weight, head_gain, out_weight, out_gain,
):
    row = lambda x: x.reshape(1, D)
    tokens, att = encode(
        field, stem_weight, kv_weight, latents, query_weight, row(stem_bias), row(token_gain), row(latent_gain), head_gain
    )
    return mix(tokens, att, out_weight, row(out_gain))


def solution(mesh):
    return jax.shard_map(
        shards,
        mesh=mesh,
        in_specs=(P(None, "lat", "lon"), P(), P(), P(), P(), P(), P(), P(), P(), P(), P()),
        out_specs=(P("lat", "lon", None), P()),
        check_vma=False,
    )
```

```python
import functools

import jax
import jax.numpy as jnp
from jax import lax
from jax.experimental import pallas as pl
from jax.experimental.pallas import tpu as pltpu
from jax.sharding import PartitionSpec as P

HEADS = 8
HD = 64
LAT = 512
D = 512
CHAN = 69
CPAD = 80
ROWS = 32
COLS = 512
TH = 16
TW = 256
TOK = TH * TW
SLAB = 4 * CPAD
NLATD = 16
NLOND = 8
EXT = 80
CH = 2048
PITCH = 40
LIMIT = 58
MESH = pl.DeviceIdType.MESH
F32 = jnp.float32
BF = jnp.bfloat16
VM = pl.BlockSpec(memory_space=pltpu.VMEM)
SM = pl.BlockSpec(memory_space=pltpu.SMEM)
ANY = pl.BlockSpec(memory_space=pl.ANY)


def remote(src, dst, send, recv, target):
    return pltpu.make_async_remote_copy(
        src_ref=src, dst_ref=dst, send_sem=send, recv_sem=recv, device_id=target, device_id_type=MESH
    )


def encode_kernel(
    field_hbm, sw_hbm, kvw_hbm, latents_hbm, qw_hbm, bias_ref, gain_ref, lgain_ref, hg_ref,
    tok_ref, out_ref,
    field_ref, sw_ref, kvw_ref, latents_ref, qw_ref,
    sl_ref, wt_ref, wvt_ref, qt_ref, g_ref, wp_ref, cols_ref, colr_ref, rowr_ref,
    affine_ref, stem_ref, turned_ref,
    k_ref, vt_ref, s_ref, mx_ref, acc_ref, src1, dst1, src2, dst2, att,
    in_sem, edge_send, edge_recv, send1, recv1, send2, recv2, send3, recv3,
):
    lat = lax.axis_index("lat")
    lon = lax.axis_index("lon")
    up, down = lax.rem(lat + NLATD - 1, NLATD), lax.rem(lat + 1, NLATD)
    left, right = lax.rem(lon + NLOND - 1, NLOND), lax.rem(lon + 1, NLOND)
    loads = [
        pltpu.make_async_copy(src, dst, in_sem.at[i])
        for i, (src, dst) in enumerate([
            (field_hbm, field_ref), (sw_hbm, sw_ref), (kvw_hbm, kvw_ref), (latents_hbm, latents_ref), (qw_hbm, qw_ref),
        ])
    ]
    loads[0].start()
    lon_peer = lambda s: (lat, lax.rem(lon + s, NLOND))
    lat_peer = lambda s: (lax.rem(lat + s, NLATD), lon)
    barrier = pltpu.get_barrier_semaphore()
    around = [(up, left), (up, right), (down, left), (down, right)]
    around += [lon_peer(s) for s in range(1, NLOND)] + [lat_peer(s) for s in range(1, NLATD)]
    for target in around:
        pl.semaphore_signal(barrier, inc=1, device_id=target, device_id_type=MESH)

    source = lax.broadcasted_iota(jnp.int32, (256, 256), 0)
    place = lax.broadcasted_iota(jnp.int32, (256, 256), 1)
    wanted = jnp.where(place < 128, 2 * place, 2 * (place - 128) + 1)
    select = (source == wanted).astype(F32).astype(BF)
    loads[0].wait()
    for load in loads[1:]:
        load.start()
    for half in range(2):
        block = field_ref[:, :, half * 256:(half + 1) * 256].reshape(CHAN * ROWS, 256)
        both = jnp.dot(block, select, preferred_element_type=F32)
        for c in range(CHAN):
            rows = both[c * ROWS:(c + 1) * ROWS]
            g_ref[half, c * PITCH:c * PITCH + ROWS, :] = rows[:, :128]
            g_ref[2 + half, c * PITCH:c * PITCH + ROWS, :] = rows[:, 128:]
    g_ref[:, CHAN * PITCH:CPAD * PITCH, :] = jnp.zeros((4, (CPAD - CHAN) * PITCH, 128), F32)

    lane = lax.broadcasted_iota(jnp.int32, (CPAD, 128), 1)

    def spread(y, carry):
        first, last = carry
        quarter = [g_ref[n, pl.ds(y, CPAD, stride=PITCH), :] for n in range(4)]
        even = jnp.concatenate(quarter[:2], axis=1)
        odd = jnp.concatenate(quarter[2:], axis=1)
        base = pl.multiple_of((y + 1) * SLAB, SLAB)
        sl_ref[pl.ds(base, CPAD), :] = pltpu.roll(odd, 1, 1).astype(BF)
        sl_ref[pl.ds(base + CPAD, CPAD), :] = even.astype(BF)
        sl_ref[pl.ds(base + 2 * CPAD, CPAD), :] = odd.astype(BF)
        sl_ref[pl.ds(base + 3 * CPAD, CPAD), :] = pltpu.roll(even, 255, 1).astype(BF)
        first = jnp.where(lane == y, pltpu.roll(even[:, :128], y, 1), first)
        last = jnp.where(lane == y, pltpu.roll(odd[:, 128:], y + 1, 1), last)
        return first, last

    empty = jnp.zeros((CPAD, 128), F32)
    first, last = lax.fori_loop(0, ROWS, spread, (empty, empty), unroll=2)
    cols_ref[0] = first.astype(BF)
    cols_ref[1] = last.astype(BF)
    pl.semaphore_wait(barrier, len(around))
    routes = [
        (cols_ref.at[1], colr_ref.at[0], (lat, right)),
        (cols_ref.at[0], colr_ref.at[1], (lat, left)),
        (cols_ref.at[1], colr_ref.at[2], (down, right)),
        (cols_ref.at[0], colr_ref.at[3], (down, left)),
        (cols_ref.at[1], colr_ref.at[4], (up, right)),
        (cols_ref.at[0], colr_ref.at[5], (up, left)),
        (sl_ref.at[pl.ds(ROWS * SLAB + CPAD, 2 * CPAD)], rowr_ref.at[0], (down, lon)),
        (sl_ref.at[pl.ds(SLAB + CPAD, 2 * CPAD)], rowr_ref.at[1], (up, lon)),
    ]
    copies = [
        remote(src, dst, edge_send.at[i], edge_recv.at[i], target)
        for i, (src, dst, target) in enumerate(routes)
    ]
    for i in (0, 1, 6, 7, 2, 3, 4, 5):
        copies[i].start()

    for load in loads[1:]:
        load.wait()
    for n in range(4):
        g_ref[n, 0:16 * CHAN, :] = sw_ref[:, n * 128:(n + 1) * 128].astype(F32)
        for q in range(16):
            part = g_ref[n, pl.ds(q * CHAN, CHAN), :]
            part = jnp.concatenate([part, jnp.zeros((CPAD - CHAN, 128), F32)], axis=0)
            wp_ref[pl.ds(q * CPAD, CPAD), n * 128:(n + 1) * 128] = part.astype(BF)
    for n, ref in enumerate((bias_ref, gain_ref)):
        affine_ref[n] = jnp.broadcast_to(ref[...], (128, D)).T
    for q in range(5):
        wt_ref[:, pl.ds(q * 256, 256)] = wp_ref[pl.ds(q * 256, 256), :].T
    wvt_ref[...] = kvw_ref[:, D:].T
    latents = latents_ref[...]
    centred = latents - jnp.mean(latents, axis=-1, keepdims=True)
    variance = jnp.mean(centred * centred, axis=-1, keepdims=True)
    normed = (centred / jnp.sqrt(variance + 1e-05) * lgain_ref[...]).astype(BF)
    query = jnp.dot(normed, qw_ref[...], preferred_element_type=F32).astype(BF)
    turned = query.T
    for h in range(HEADS):
        mine = (h % 2) * HD
        qt_ref[h, mine:mine + HD, :] = turned[h * HD:(h + 1) * HD, :]
        qt_ref[h, HD - mine:2 * HD - mine, :] = jnp.zeros((HD, LAT), BF)

    for copy in copies[:2]:
        copy.wait()

    def patch(y, left_column, right_column, left_roll, right_roll, base):
        a = sl_ref[pl.ds(base, CPAD), 0:128].astype(F32)
        b = sl_ref[pl.ds(base + 3 * CPAD, CPAD), 128:256].astype(F32)
        low = pltpu.roll(left_column.astype(F32), left_roll, 1)
        high = pltpu.roll(right_column.astype(F32), right_roll, 1)
        sl_ref[pl.ds(base, CPAD), 0:128] = jnp.where(lane == 0, low, a).astype(BF)
        sl_ref[pl.ds(base + 3 * CPAD, CPAD), 128:256] = jnp.where(lane == 127, high, b).astype(BF)

    def mend(y, carry):
        base = pl.multiple_of((y + 1) * SLAB, SLAB)
        patch(y, colr_ref[0], colr_ref[1], lax.rem(128 - y, 128), 127 - y, base)
        return carry

    lax.fori_loop(0, ROWS, mend, 0, unroll=4)

    def stem(r, slot):
        window = sl_ref[pl.ds(pl.multiple_of(r * 2 * SLAB, 2 * SLAB), 4 * SLAB), :]
        stem_ref[slot] = jnp.dot(wt_ref[...], window, preferred_element_type=F32)

    def norm(r, slot):
        wide = lambda n: jnp.concatenate([affine_ref[n]] * 2, axis=1)
        value = stem_ref[slot] + wide(0)
        centred = value - jnp.mean(value, axis=0, keepdims=True)
        variance = jnp.mean(centred * centred, axis=0, keepdims=True)
        turned = (centred * (1.0 / jnp.sqrt(variance + 1e-05)) * wide(1)).astype(BF)
        turned_ref[slot] = turned
        tok_ref[r] = turned.T

    def project(r, slot):
        at = pl.ds(pl.multiple_of(r * TW, TW), TW)
        keys = jnp.dot(tok_ref[r], kvw_ref[:, 0:D], preferred_element_type=F32).astype(BF)
        for pair in range(HEADS // 2):
            k_ref[pair, at, :] = keys[:, pair * 128:(pair + 1) * 128]
        values = jnp.dot(wvt_ref[...], turned_ref[slot], preferred_element_type=F32).astype(BF)
        for h in range(HEADS):
            vt_ref[h, 0:HD, at] = values[h * HD:(h + 1) * HD, :]
            vt_ref[h, HD:EXT, at] = jnp.ones((EXT - HD, TW), BF)

    def border():
        for copy in copies[2:]:
            copy.wait()
        for index, (slab, y, inside) in enumerate([(0, ROWS - 1, lat > 0), (ROWS + 1, 0, lat < NLATD - 1)]):
            base = slab * SLAB
            keep = jnp.where(inside, 1.0, 0.0).astype(F32)
            even = rowr_ref[index, 0:CPAD, :].astype(F32) * keep
            odd = rowr_ref[index, CPAD:2 * CPAD, :].astype(F32) * keep
            sl_ref[pl.ds(base, CPAD), :] = pltpu.roll(odd, 1, 1).astype(BF)
            sl_ref[pl.ds(base + CPAD, CPAD), :] = even.astype(BF)
            sl_ref[pl.ds(base + 2 * CPAD, CPAD), :] = odd.astype(BF)
            sl_ref[pl.ds(base + 3 * CPAD, CPAD), :] = pltpu.roll(even, 255, 1).astype(BF)
            patch(
                y, colr_ref[2 + 2 * index].astype(F32) * keep, colr_ref[3 + 2 * index].astype(F32) * keep,
                (128 - y) % 128, 127 - y, base,
            )

    stem(1, 1)
    norm(1, 1)
    stem(2, 0)

    def two(i, carry):
        r = 2 * i + 1
        project(r, 1)
        norm(r + 1, 0)
        stem(r + 2, 1)
        project(r + 1, 0)
        norm(r + 2, 1)
        stem(r + 3, 0)
        return carry

    lax.fori_loop(0, 6, two, 0)
    border()
    project(13, 1)
    norm(14, 0)
    stem(15, 1)
    project(14, 0)
    norm(15, 1)
    stem(0, 0)
    project(15, 1)
    norm(0, 0)
    project(0, 0)

    log2e = 1.4426950408889634
    scale = lambda h: hg_ref[h] * (log2e / 8.0)

    def score(h, j):
        at = pl.ds(pl.multiple_of(j * CH, CH), CH)
        s = jnp.dot(k_ref[h // 2, at, :], qt_ref[h], preferred_element_type=F32)
        s_ref[h % 2, at, :] = s
        mx_ref[h % 2] = jnp.maximum(mx_ref[h % 2], jnp.max(s.reshape(CH // 8, 8, LAT), axis=0))

    def weigh(h, j, top):
        at = pl.ds(pl.multiple_of(j * CH, CH), CH)
        p = jnp.exp2(s_ref[h % 2, at, :] * scale(h) - top).astype(BF)
        acc_ref[...] += jnp.dot(vt_ref[h, :, at], p, preferred_element_type=F32)

    def stat_rows(top, total):
        row = lax.broadcasted_iota(jnp.int32, (16, 128), 0)
        high = total.astype(BF).astype(F32)
        out = jnp.zeros((16, 128), F32)
        for n, value in enumerate((top, high, total - high)):
            out = jnp.where(row == 2 * n, value[:, :128], out)
            out = jnp.where(row == 2 * n + 1, value[:, 128:], out)
        return out.astype(BF)

    def merge(buffer, h, count):
        stats = [buffer[h, s, :, 256:384].astype(F32) for s in range(count)]
        tops = [jnp.concatenate([x[0:1], x[1:2]], axis=1) for x in stats]
        totals = [jnp.concatenate([x[2:3] + x[4:5], x[3:4] + x[5:6]], axis=1) for x in stats]
        top = functools.reduce(jnp.maximum, tops)
        total = jnp.zeros((1, 256), F32)
        acc = jnp.zeros((16, 256), F32)
        for s in range(count):
            fold = jnp.exp2(tops[s] - top)
            total = total + totals[s] * fold
            acc = acc + buffer[h, s, :, 0:256].astype(F32) * fold
        return top, total, acc

    def stage1(h, top):
        acc = acc_ref[...]
        total = acc[HD:HD + 1, :]
        stats = [stat_rows(top[:, g * 256:(g + 1) * 256], total[:, g * 256:(g + 1) * 256]) for g in range(2)]
        for p in range(NLOND):
            e, g = p % 4, p // 4
            src1[h, p, :, 0:256] = acc[16 * e:16 * e + 16, g * 256:(g + 1) * 256].astype(BF)
            src1[h, p, :, 256:384] = stats[g]
        dst1[h, 0] = src1[h, lon]
        for s in range(1, NLOND):
            remote(src1.at[h, lax.rem(lon + s, NLOND)], dst1.at[h, s], send1.at[h], recv1.at[h], lon_peer(s)).start()

    def wait(ref, sem):
        pltpu.make_async_copy(ref, ref, sem).wait()

    def stage2(h):
        wait(dst1.at[h, pl.ds(1, NLOND - 1)], recv1.at[h])
        top, total, acc = merge(dst1, h, NLOND)
        stats = stat_rows(top, total)
        src2[h, :, 0:256] = acc.astype(BF)
        src2[h, :, 256:384] = stats
        dst2[h, lat, :, 0:256] = acc.astype(BF)
        dst2[h, lat, :, 256:384] = stats
        for s in range(1, NLATD):
            remote(src2.at[h], dst2.at[h, lat], send2.at[h], recv2.at[h], lat_peer(s)).start()

    e_at = lax.rem(lon, 4) * 16
    g_at = pl.multiple_of(lon // 4 * 256, 256)

    def stage3(h):
        wait(dst2.at[h, pl.ds(1, NLATD - 1)], recv2.at[h])
        top, total, acc = merge(dst2, h, NLATD)
        here = att.at[pl.ds(pl.multiple_of(h * HD + e_at, 16), 16), pl.ds(g_at, 256)]
        here[...] = (acc / total).astype(BF)
        for s in range(1, NLOND):
            remote(here, here, send3.at[h], recv3.at[h], lon_peer(s)).start()

    for h in range(HEADS + 1):
        slot = h % 2
        if h < HEADS:
            mx_ref[slot] = jnp.full((8, LAT), -jnp.inf, F32)
        if h > 0:
            peak = jnp.max(mx_ref[1 - slot], axis=0, keepdims=True) * scale(h - 1)
            top = (peak + jnp.abs(peak) * 2.0**-7).astype(BF).astype(F32)
            acc_ref[...] = jnp.zeros_like(acc_ref)

        def both(j, carry):
            if h < HEADS:
                score(h, j)
            if h > 0:
                weigh(h - 1, j, top)
            return carry

        lax.fori_loop(0, TOK // CH, both, 0)
        if h > 0:
            stage1(h - 1, top)
        if h > 2:
            stage2(h - 3)
        if h > 5:
            stage3(h - 6)
    stage2(6)
    stage3(3)
    stage3(4)
    stage2(7)
    stage3(5)
    stage3(6)
    stage3(7)
    for h in range(HEADS):
        wait(att.at[pl.ds(0, 112), pl.ds(0, 256)], recv3.at[h])
        wait(dst1.at[h, pl.ds(1, NLOND - 1)], send1.at[h])
        wait(dst2.at[h, pl.ds(1, NLATD - 1)], send2.at[h])
        wait(att.at[pl.ds(0, 112), pl.ds(0, 256)], send3.at[h])
    out_ref[...] = att[...]


def encode(field, sw, kvw, latents, qw, bias, gain, lgain, hg):
    dma = pltpu.SemaphoreType.DMA
    return pl.pallas_call(
        encode_kernel,
        out_shape=(pltpu.VMEM((TH, TW, D), BF), pltpu.VMEM((D, LAT), BF)),
        in_specs=[ANY] * 5 + [VM] * 3 + [SM],
        out_specs=(VM, VM),
        scratch_shapes=[
            pltpu.VMEM((CHAN, ROWS, COLS), BF),
            pltpu.VMEM((16 * CHAN, D), BF),
            pltpu.VMEM((D, 2 * D), BF),
            pltpu.VMEM((LAT, D), F32),
            pltpu.VMEM((D, D), BF),
            pltpu.VMEM(((ROWS + 2) * SLAB, TW), BF),
            pltpu.VMEM((D, 16 * CPAD), BF),
            pltpu.VMEM((D, D), BF),
            pltpu.VMEM((HEADS, 2 * HD, LAT), BF),
            pltpu.VMEM((4, CPAD * PITCH, 128), F32),
            pltpu.VMEM((16 * CPAD, D), BF),
            pltpu.VMEM((2, CPAD, 128), BF),
            pltpu.VMEM((6, CPAD, 128), BF),
            pltpu.VMEM((2, 2 * CPAD, TW), BF),
            pltpu.VMEM((2, D, 128), F32),
            pltpu.VMEM((2, D, TW), F32),
            pltpu.VMEM((2, D, TW), BF),
            pltpu.VMEM((HEADS // 2, TOK, 128), BF),
            pltpu.VMEM((HEADS, EXT, TOK), BF),
            pltpu.VMEM((2, TOK, LAT), F32),
            pltpu.VMEM((2, 8, LAT), F32),
            pltpu.VMEM((EXT, LAT), F32),
            pltpu.VMEM((HEADS, NLOND, 16, 384), BF),
            pltpu.VMEM((HEADS, NLOND, 16, 384), BF),
            pltpu.VMEM((HEADS, 16, 384), BF),
            pltpu.VMEM((HEADS, NLATD, 16, 384), BF),
            pltpu.VMEM((D, LAT), BF),
            dma((5,)), dma((8,)), dma((8,)),
        ] + [dma((HEADS,))] * 6,
        compiler_params=pltpu.CompilerParams(
            collective_id=0, has_side_effects=True, vmem_limit_bytes=LIMIT * 2**20
        ),
        name="encode",
    )(field, sw, kvw, latents, qw, bias, gain, lgain, hg)


def mix_kernel(tok_in, att_ref, ow_ref, gain_ref, tok_out, out_ref, sem):
    copies = [pltpu.make_async_copy(tok_in.at[pl.ds(4 * n, 4)], tok_out.at[pl.ds(4 * n, 4)], sem.at[n]) for n in range(4)]
    for copy in copies:
        copy.start()
    weight = ow_ref[...]
    for n in range(4):
        mixed = lax.dot_general(
            att_ref[:, n * 128:(n + 1) * 128], weight, (((0,), (0,)), ((), ())), preferred_element_type=F32
        )
        centred = mixed - jnp.mean(mixed, axis=-1, keepdims=True)
        variance = jnp.mean(centred * centred, axis=-1, keepdims=True)
        out_ref[n * 128:(n + 1) * 128, :] = centred / jnp.sqrt(variance + 1e-05) * gain_ref[...]
    for copy in copies:
        copy.wait()


def mix(tokens, att, ow, gain):
    return pl.pallas_call(
        mix_kernel,
        out_shape=(jax.ShapeDtypeStruct((TH, TW, D), BF), jax.ShapeDtypeStruct((LAT, D), F32)),
        in_specs=[ANY] + [VM] * 3,
        out_specs=(ANY, VM),
        scratch_shapes=[pltpu.SemaphoreType.DMA((4,))],
        compiler_params=pltpu.CompilerParams(vmem_limit_bytes=12 * 2**20),
        name="mix",
    )(tokens, att, ow, gain)


def shards(
    field, stem_weight, stem_bias, token_gain, kv_weight, latents, latent_gain,
    query_weight, head_gain, out_weight, out_gain,
):
    row = lambda x: x.reshape(1, D)
    tokens, att = encode(
        field, stem_weight, kv_weight, latents, query_weight, row(stem_bias), row(token_gain), row(latent_gain), head_gain
    )
    return mix(tokens, att, out_weight, row(out_gain))


def solution(mesh):
    return jax.shard_map(
        shards,
        mesh=mesh,
        in_specs=(P(None, "lat", "lon"), P(), P(), P(), P(), P(), P(), P(), P(), P(), P()),
        out_specs=(P("lat", "lon", None), P()),
        check_vma=False,
    )
```
